32 devices in a mesh: row: 8 (over z, x), sub: 4 (over y, core).
Axes of the slice: x: 2, y: 2, z: 4, core: 2. Of those that a mesh axis runs over, the one named last changes fastest.
Arguments:
- blocks: bfloat16 [256, 512, 512], P(('row', 'sub')), may hold values from 0.099 to 10
- blk_row: int32 [256], P(('row', 'sub')), may hold values from 0 to 63, as said below
- blk_col: int32 [256], P(('row', 'sub')), may hold values from 0 to 63, as said below
- counts: int32 [32], P(('row', 'sub')), may hold values from 0 to 8, as said below
- bias: float32 [32768], P(('row', 'sub')), may hold values from 0.3 to 5.1
- mask: int32 [32768], P(('row', 'sub')), may hold values 0 or 1
Outputs:
- balanced: float32 [32768], P(('row', 'sub'))
- coverage: float32 [32768], P(('row', 'sub'))
The draws below stay inside these ranges and needn't reach their ends.
Inputs may be any that keep to these rules, and one draw needn't show every extreme that they name: blk_col equals blk_row or blk_row + 1. Among the live slots of the 4 devices of row group g, every pair (p, p) and (p, p + 1) with g * 8 <= p < (g + 1) * 8 and p + 1 < 64 stands exactly once, and no other pair; every slot, live or not, names a block row of its own group. `blk_col`: block column of each slot, as described for blk_row. `counts`: in every row group one device holds exactly 8 live slots.
All inputs are finite; a program needn't handle non-finite values. No bound on the sum of `mask` on one device may be relied on, other than what follows from the above.
Results may differ from the reference program's by a relative error of at most 0.0003.
Values sent between devices are 32-bit elements; how exact they have to be, the bound alone decides.
A program may use at most 64 MiB of HBM per device.

```python
import jax
import jax.numpy as jnp
from jax import lax

BLK = 512
ROWBLK = 8
ITERS = 3
NBINS = 32768
SLOTS = 256
N_ROW = 8
N_SUB = 4


def band_layout(key):
    key_order, key_full, key_cuts = jax.random.split(jax.random.fold_in(key, 11), 3)
    pairs = 2 * ROWBLK
    position = jnp.arange(pairs, dtype=jnp.int32)[None, :]
    groups = jnp.arange(N_ROW, dtype=jnp.int32)[:, None]
    rows_all = groups * ROWBLK + position % ROWBLK
    cols_all = rows_all + (position >= ROWBLK).astype(jnp.int32)
    valid = (cols_all < ROWBLK * N_ROW).astype(jnp.int32)
    scores = jax.random.randint(key_order, (N_ROW, pairs), 0, 65536, dtype=jnp.int32) * pairs + position + (1 - valid) * 268435456
    order = jnp.argsort(scores, axis=1)
    rows_sorted = jnp.take_along_axis(rows_all, order, axis=1)
    cols_sorted = jnp.take_along_axis(cols_all, order, axis=1)
    rest = jnp.sum(valid, axis=1) - ROWBLK
    fuller = jax.random.randint(key_full, (N_ROW,), 0, N_SUB, dtype=jnp.int32)
    pieces = jax.random.randint(key_cuts, (N_ROW, N_SUB - 1), 1, 9, dtype=jnp.int32)
    running = jnp.cumsum(pieces, axis=1)
    cuts = rest[:, None] * running // running[:, -1:]
    others = cuts - jnp.concatenate([jnp.zeros((N_ROW, 1), jnp.int32), cuts[:, :-1]], axis=1)
    starts_other = ROWBLK + cuts - others
    subs = jnp.arange(N_SUB, dtype=jnp.int32)[None, :]
    rank = jnp.clip(subs - (subs > fuller[:, None]).astype(jnp.int32), 0, N_SUB - 2)
    is_full = subs == fuller[:, None]
    live_counts = jnp.where(is_full, ROWBLK, jnp.take_along_axis(others, rank, axis=1))
    starts = jnp.where(is_full, 0, jnp.take_along_axis(starts_other, rank, axis=1))
    slot = jnp.arange(ROWBLK, dtype=jnp.int32)[None, None, :]
    place = jnp.clip(starts[:, :, None] + slot, 0, pairs - 1)
    active = slot < live_counts[:, :, None]
    row_slots = jnp.take_along_axis(jnp.broadcast_to(rows_sorted[:, None, :], (N_ROW, N_SUB, pairs)), place, axis=2)
    col_slots = jnp.take_along_axis(jnp.broadcast_to(cols_sorted[:, None, :], (N_ROW, N_SUB, pairs)), place, axis=2)
    own_first = groups[:, :, None] * ROWBLK
    blk_row = jnp.where(active, row_slots, own_first).reshape(-1).astype(jnp.int32)
    blk_col = jnp.where(active, col_slots, own_first).reshape(-1).astype(jnp.int32)
    return (blk_row, blk_col, live_counts.reshape(-1).astype(jnp.int32))


def draw_blk_row(key, part):
    return band_layout(key)[0]


def draw_blk_col(key, part):
    return band_layout(key)[1]


def draw_counts(key, part):
    return band_layout(key)[2]


def draw_blocks(key, part):
    key_level = jax.random.fold_in(jax.random.fold_in(key, 23), 0)
    key_fine = jax.random.fold_in(jax.random.fold_in(key, 23), 3)
    levels = jax.random.uniform(key_level, (SLOTS, 1, 1), jnp.float32, -1.5, 1.5)
    fine_noise = jax.random.uniform(key_fine, (SLOTS, BLK, BLK), jnp.float32, -1.15, 1.15)
    log_values = levels + fine_noise
    return jnp.clip(jnp.exp(log_values), 0.1, 10.0).astype(jnp.bfloat16)


def draw_bias(key, part):
    position = jnp.arange(NBINS, dtype=jnp.float32) / NBINS
    spread = jax.random.uniform(key, (NBINS,), jnp.float32, -0.8, 0.8)
    return jnp.exp(spread) * jnp.sqrt(1.0 + 2.0 * position)


def set_ends(drawn, rng, least, largest):
    longest = drawn.shape.index(max(drawn.shape))
    spots = []
    for shift in (0, 1):
        where = [jax.random.randint(jax.random.fold_in(rng, axis), (), 0, length) for axis, length in enumerate(drawn.shape)]
        where[longest] = (where[longest] + shift) % drawn.shape[longest]
        spots.append(tuple(where))
    return drawn.at[spots[0]].set(least).at[spots[1]].set(largest)


def setup_inputs(seed: int = 0) -> dict:
    keys = jax.random.split(jax.random.key(seed), 7)
    blocks = draw_blocks(jax.random.fold_in(keys[6], 71), 0)
    blk_row = draw_blk_row(jax.random.fold_in(keys[6], 71), 0)
    blk_col = draw_blk_col(jax.random.fold_in(keys[6], 71), 0)
    counts = draw_counts(jax.random.fold_in(keys[6], 71), 0)
    bias = draw_bias(jax.random.fold_in(keys[6], 71), 0)
    mask = set_ends((jax.random.randint(keys[5], (NBINS,), 0, 10) < 9).astype(jnp.int32), jax.random.fold_in(keys[5], 1), 0, 1)
    return dict(blocks=blocks, blk_row=blk_row, blk_col=blk_col, counts=counts, bias=bias, mask=mask)


def reference(blocks, blk_row, blk_col, counts, bias, mask):
    live = mask.astype(jnp.float32)
    weights_now = bias * live
    live_bins = jnp.sum(live)
    coverage = jnp.zeros_like(weights_now)
    for repeat in range(ITERS):
        padded = jnp.concatenate([weights_now, jnp.zeros((BLK,), weights_now.dtype)])

        def accumulate(slot, running):
            device = slot // ROWBLK
            active = (slot % ROWBLK) < counts[device]
            row_block = blk_row[slot].astype(jnp.int32)
            col_block = blk_col[slot].astype(jnp.int32)
            factor = jnp.where(active, jnp.where(row_block == col_block, 0.5, 1.0), 0.0).astype(padded.dtype)
            block = lax.dynamic_index_in_dim(blocks, slot, 0, keepdims=False).astype(padded.dtype)
            row_bias = lax.dynamic_slice_in_dim(padded, row_block * BLK, BLK)
            col_bias = lax.dynamic_slice_in_dim(padded, col_block * BLK, BLK)
            row_terms = jnp.dot(block, col_bias, precision=lax.Precision.HIGHEST)
            col_terms = jnp.dot(row_bias, block, precision=lax.Precision.HIGHEST)
            current = lax.dynamic_slice_in_dim(running, row_block * BLK, BLK)
            running = lax.dynamic_update_slice_in_dim(running, current + factor * row_terms, row_block * BLK, 0)
            current = lax.dynamic_slice_in_dim(running, col_block * BLK, BLK)
            running = lax.dynamic_update_slice_in_dim(running, current + factor * col_terms, col_block * BLK, 0)
            return running

        sums = lax.fori_loop(0, SLOTS, accumulate, jnp.zeros_like(padded))
        scaled = weights_now * sums[:NBINS]
        average = jnp.sum(scaled) / live_bins
        coverage = scaled / average
        weights_now = weights_now * live / (coverage + 1.0 - live)
    return weights_now, coverage
```

```python
import functools

import jax
import jax.numpy as jnp
from jax import lax
from jax.experimental import pallas as pl
from jax.experimental.pallas import tpu as pltpu
from jax.sharding import PartitionSpec as P

BLK = 512
ITERS = 3
LANES = 128
PIECES = BLK // LANES
TILE = 8
PAD = 16
LEAD = TILE


def kernel(
    row_hbm, col_hbm, count_hbm, bias_hbm, mask_hbm, blocks_ref, both_ref,
    row_ref, col_ref, count_ref, bias_ref, mask_ref, held, turned, weights, follow, part, peers, before, after, last_peers, last_before, sums_out, sums_in, mask_a, mask_c, mask_r,
    small_sem, load_sem, gather_send, gather_recv, edge_send, edge_recv, peer_send, peer_recv,
    before_send, before_recv, after_send, after_recv, sums_send, sums_recv,
):
    rows, subs = lax.axis_size("row"), lax.axis_size("sub")
    devices = rows * subs
    row, sub = lax.axis_index("row"), lax.axis_index("sub")
    me = row * subs + sub
    slots = held.shape[0]
    own = bias_ref.shape[0]
    group = own * subs
    span = group + TILE
    has_before, has_after = row > 0, row < rows - 1

    def remote(src, dst, send, recv, target_row, target_sub):
        return pltpu.make_async_remote_copy(
            src_ref=src, dst_ref=dst, send_sem=send, recv_sem=recv,
            device_id=(target_row, target_sub), device_id_type=pl.DeviceIdType.MESH,
        )

    def wait_bytes(ref, sem):
        pltpu.make_async_copy(ref, ref, sem).wait()

    def ring(offset):
        return lax.rem(sub + offset, subs)

    loads = [pltpu.make_async_copy(blocks_ref.at[s], held.at[s], load_sem.at[s]) for s in range(slots)]
    smalls = [
        pltpu.make_async_copy(src, dst, small_sem.at[i])
        for i, (src, dst) in enumerate(
            ((bias_hbm, bias_ref), (mask_hbm, mask_ref), (row_hbm, row_ref), (col_hbm, col_ref), (count_hbm, count_ref))
        )
    ]
    for load in smalls + loads:
        load.start()
    barrier = pltpu.get_barrier_semaphore()

    @pl.loop(1, devices)
    def _(offset):
        target = lax.rem(me + offset, devices)
        pl.semaphore_signal(
            barrier, inc=1, device_id=(target // subs, lax.rem(target, subs)), device_id_type=pl.DeviceIdType.MESH
        )

    for load in smalls:
        load.wait()
    first_block = row * (group // PIECES)
    ids = lax.broadcasted_iota(jnp.int32, (PAD, LANES), 0)
    edge = [
        jnp.where(
            jnp.logical_and(
                s < count_ref[0],
                jnp.logical_or(row_ref[s] == first_block, col_ref[s] == first_block + group // PIECES),
            ),
            1,
            0,
        )
        for s in range(slots)
    ]
    inner_total = slots - sum(edge)
    order = [0] * slots
    inner_seen, edge_seen = 0, 0
    for s in range(slots):
        place = jnp.where(edge[s] == 1, inner_total + edge_seen, inner_seen)
        for i in range(slots):
            order[i] = order[i] + jnp.where(place == i, s, 0)
        inner_seen = inner_seen + 1 - edge[s]
        edge_seen = edge_seen + edge[s]
    for s in range(slots):
        p = row_ref[order[s]] - first_block
        q = col_ref[order[s]] - first_block
        alive = jnp.where(order[s] < count_ref[0], 1.0, 0.0).astype(jnp.float32)
        same = jnp.where(p == q, 1.0, 0.0).astype(jnp.float32)
        at_p = jnp.where(ids == p, 1.0, 0.0).astype(jnp.float32)
        at_q = jnp.where(ids == q, 1.0, 0.0).astype(jnp.float32)
        for ref, value in (
            (mask_a, at_p * (0.5 * alive * same)),
            (mask_c, at_q * (alive * (1.0 - same))),
            (mask_r, at_p * (alive * (1.0 - same))),
        ):
            value = value.astype(jnp.bfloat16)
            ref[s] = jnp.concatenate([value, value], axis=0)
    weights[0:LEAD, :] = jnp.zeros((LEAD, LANES), jnp.float32)
    rest = weights.shape[0] - LEAD - group
    weights[LEAD + group :, :] = jnp.zeros((rest, LANES), jnp.float32)

    @pl.when(jnp.logical_not(has_after))
    def _():
        follow[...] = jnp.zeros_like(follow)
        after[...] = jnp.zeros_like(after)

    @pl.when(jnp.logical_not(has_before))
    def _():
        before[...] = jnp.zeros_like(before)
        last_before[...] = jnp.zeros_like(last_before)

    @pl.when(jnp.logical_and(has_before, sub > 0))
    def _():
        last_before[...] = jnp.zeros_like(last_before)

    own_live = mask_ref[...].astype(jnp.float32)
    mine = pl.ds(pl.multiple_of(LEAD + sub * own, TILE), own)
    weights[mine, :] = bias_ref[...] * own_live

    for s in range(0, slots // 2):
        loads[s].wait()
        turned[s] = held[s].T

    pl.semaphore_wait(barrier, devices - 1)

    @pl.when(jnp.logical_and(has_before, sub == 0))
    def _():
        for target in range(subs):
            remote(
                weights.at[pl.ds(LEAD, TILE)], follow,
                edge_send.at[target], edge_recv, row - 1, target,
            ).start()

    for offset in range(1, subs):
        remote(
            weights.at[mine], weights.at[mine], gather_send.at[offset - 1], gather_recv.at[offset - 1], row, ring(offset)
        ).start()

    for s in range(slots // 2, slots):
        loads[s].wait()
        turned[s] = held[s].T

    for offset in range(1, subs):
        theirs = weights.at[pl.ds(pl.multiple_of(LEAD + ring(subs - offset) * own, TILE), own)]
        wait_bytes(theirs, gather_recv.at[offset - 1])

    top = lax.broadcasted_iota(jnp.int32, (TILE, LANES), 0) < PIECES
    current = weights[LEAD : LEAD + group, :]
    alive = current > 0.0
    totals = []
    lane = lax.broadcasted_iota(jnp.int32, (1, LANES), 1)
    kept = jnp.sum(jnp.sum(own_live, axis=0, keepdims=True), axis=1, keepdims=True)

    def operand(start):
        value = jnp.concatenate(
            [weights[pl.ds(LEAD + start + q, PAD, stride=PIECES), :] for q in range(PIECES)], axis=1
        )
        high = value.astype(jnp.bfloat16)
        low = (value - high.astype(jnp.float32)).astype(jnp.bfloat16)
        return jnp.concatenate([high, low], axis=0)

    def wide(mask):
        return jnp.concatenate([mask] * PIECES, axis=1)

    edges = min(3, slots)
    state = {}

    def edge_weights(k):
        if k == 0:

            @pl.when(has_after)
            def _():
                wait_bytes(follow, edge_recv)

            back = jnp.where(top, follow[...], 0.0)
            state["back_live"] = back > 0.0
            state["whole"] = jnp.concatenate([current, back], axis=0)
        else:

            @pl.when(has_before)
            def _():
                wait_bytes(before.at[k - 1], before_recv.at[k - 1])

            @pl.when(has_after)
            def _():
                wait_bytes(after.at[k - 1], after_recv.at[k - 1])

            sums = state["sums"]
            front = sums[:TILE] + jnp.where(top, jnp.sum(before[k - 1], axis=0), 0.0)
            back = sums[group:] + jnp.sum(after[k - 1], axis=0)
            front = jnp.where(alive[:TILE], 1.0 / front, 0.0)
            back = jnp.where(state["back_live"], 1.0 / back, 0.0)
            weights[LEAD : LEAD + TILE, :] = front
            state["whole"] = jnp.concatenate([front, state["inner"][TILE:], back], axis=0)
        weights[LEAD + group : LEAD + span, :] = back

    for k in range(ITERS):
        total = jnp.zeros((2 * PAD, BLK), jnp.float32)
        for s in range(slots):
            if s == 0:
                here, lower, upper = operand(0), operand(-PIECES), operand(PIECES)
            if s == slots - edges:
                edge_weights(k)
                here, lower, upper = operand(0), operand(-PIECES), operand(PIECES)
            on = wide(mask_a[s]) * here
            left_c = on + wide(mask_c[s]) * lower
            left_r = on + wide(mask_r[s]) * upper
            total += lax.dot_general(left_c, held[order[s]], (((1,), (0,)), ((), ())), preferred_element_type=jnp.float32)
            total += lax.dot_general(left_r, turned[order[s]], (((1,), (0,)), ((), ())), preferred_element_type=jnp.float32)
        total = total[:PAD] + total[PAD:]
        for q in range(PIECES):
            part[k, pl.ds(q, PAD, stride=PIECES), :] = total[:, q * LANES : (q + 1) * LANES]
        final = k == ITERS - 1
        edge_rows = pl.ds(group, TILE)
        if not final:
            @pl.when(has_after)
            def _():
                for offset in range(subs):
                    remote(
                        part.at[k, edge_rows], before.at[k, offset], before_send.at[k], before_recv.at[k],
                        row + 1, ring(offset),
                    ).start()

            @pl.when(has_before)
            def _():
                for offset in range(subs):
                    remote(
                        part.at[k, pl.ds(0, TILE)], after.at[k, offset], after_send.at[k], after_recv.at[k],
                        row - 1, ring(offset),
                    ).start()

            for offset in range(1, subs):
                remote(
                    part.at[k, pl.ds(0, span)], peers.at[k, offset - 1],
                    peer_send.at[k], peer_recv.at[k], row, ring(offset),
                ).start()

            product = state["whole"] * part[k, 0:span, :]
            totals.append(jnp.sum(jnp.sum(product, axis=0, keepdims=True), axis=1, keepdims=True))
            wait_bytes(peers.at[k], peer_recv.at[k])
            sums = part[k, 0:span, :]
            for offset in range(1, subs):
                sums += peers[k, offset - 1]
            state["sums"] = sums
            state["inner"] = jnp.where(alive, 1.0 / sums[:group], 0.0)
            if k == 0:
                for offset in range(1, subs):
                    wait_bytes(weights.at[mine], gather_send.at[offset - 1])

                @pl.when(jnp.logical_and(has_before, sub == 0))
                def _():
                    for target in range(subs):
                        wait_bytes(weights.at[pl.ds(LEAD, TILE)], edge_send.at[target])

            weights[LEAD : LEAD + group, :] = state["inner"]
            weights[LEAD + group : LEAD + span, :] = jnp.zeros((TILE, LANES), jnp.float32)
        else:
            product = state["whole"] * part[k, 0:span, :]
            last = jnp.sum(product, axis=0, keepdims=True)
            half = LANES // 2
            message = last + pltpu.roll(last, half, 1)
            for i, value in enumerate(totals + [kept]):
                message = jnp.where(lane == half + i, value, message)
            message = jnp.where(lane > half + ITERS - 1, 0.0, message)
            sums_out[...] = message

            @pl.loop(0, rows)
            def _(turn):
                target_row = lax.rem(2 * rows + turn - 2 - row, rows)
                for offset in range(subs):

                    @pl.when(jnp.logical_or(target_row != row, offset != 0))
                    def _():
                        remote(
                            sums_out, sums_in.at[turn * subs + offset], sums_send, sums_recv, target_row, ring(offset)
                        ).start()

            for offset in range(1, subs):
                theirs = pl.ds(pl.multiple_of(ring(offset) * own, TILE), own)
                remote(
                    part.at[k, theirs], last_peers.at[offset - 1], peer_send.at[k], peer_recv.at[k], row, ring(offset)
                ).start()

            @pl.when(has_after)
            def _():
                remote(
                    part.at[k, edge_rows], last_before.at[sub], before_send.at[k], before_recv.at[k], row + 1, 0
                ).start()

            wait_bytes(last_peers, peer_recv.at[k])

            @pl.when(jnp.logical_and(has_before, sub == 0))
            def _():
                wait_bytes(last_before, before_recv.at[k])

            sums = part[k, pl.ds(pl.multiple_of(sub * own, TILE), own), :] + jnp.sum(last_peers[...], axis=0)
            front = jnp.where(top, jnp.sum(last_before[...], axis=0), 0.0)
            if own > TILE:
                front = jnp.concatenate([front, jnp.zeros((own - TILE, LANES), jnp.float32)], axis=0)
            sums = sums + front
            everyone = sums_in.at[pl.ds(0, devices - 1)]
            wait_bytes(everyone, sums_recv)
            self_turn = lax.rem(2 * row + 2, rows)
            sums_in[self_turn * subs] = message
            grand = jnp.sum(sums_in[...], axis=0)
            half_sum = jnp.sum(jnp.where(lane < half, grand, 0.0), axis=1, keepdims=True)
            bins = grand[:, half + ITERS - 1 : half + ITERS]
            average = half_sum / bins
            scale = average
            for i in range(ITERS - 1):
                scale = scale * (grand[:, half + i : half + i + 1] / bins)
            now = weights[mine, :]
            both_ref[1] = now * sums / average
            both_ref[0] = jnp.where(own_live > 0.0, scale / sums, 0.0)

    for k in range(ITERS):
        final = k == ITERS - 1
        wait_bytes(last_peers if final else peers.at[k], peer_send.at[k])

        @pl.when(has_after)
        def _():
            wait_bytes(last_before.at[0] if final else before.at[k], before_send.at[k])

        if not final:

            @pl.when(has_before)
            def _():
                wait_bytes(after.at[k], after_send.at[k])

    wait_bytes(sums_in.at[pl.ds(0, devices - 1)], sums_send)


def shards(blocks, blk_row, blk_col, counts, bias, mask):
    rows, subs = lax.axis_size("row"), lax.axis_size("sub")
    slots = blocks.shape[0]
    own = bias.shape[0] // LANES
    group = own * subs
    span = group + TILE
    mid = ITERS - 1
    f32, bf16 = jnp.float32, jnp.bfloat16
    dma = pltpu.SemaphoreType.DMA
    vmem = pl.BlockSpec(memory_space=pltpu.VMEM)
    def pin(x):
        return pltpu.with_memory_space_constraint(x, pltpu.HBM)

    both = pl.pallas_call(
        kernel,
        out_shape=pltpu.VMEM((2, own, LANES), f32),
        in_specs=[pl.BlockSpec(memory_space=pltpu.HBM)] * 6,
        out_specs=vmem,
        scratch_shapes=[
            pltpu.SMEM((slots,), jnp.int32),
            pltpu.SMEM((slots,), jnp.int32),
            pltpu.SMEM((1,), jnp.int32),
            pltpu.VMEM((own, LANES), f32),
            pltpu.VMEM((own, LANES), jnp.int32),
            pltpu.VMEM(blocks.shape, bf16),
            pltpu.VMEM(blocks.shape, bf16),
            pltpu.VMEM((LEAD + PAD * PIECES + TILE, LANES), f32),
            pltpu.VMEM((TILE, LANES), f32),
            pltpu.VMEM((ITERS, PAD * PIECES, LANES), f32),
            pltpu.VMEM((mid, subs - 1, span, LANES), f32),
            pltpu.VMEM((mid, subs, TILE, LANES), f32),
            pltpu.VMEM((mid, subs, TILE, LANES), f32),
            pltpu.VMEM((subs - 1, own, LANES), f32),
            pltpu.VMEM((subs, TILE, LANES), f32),
            pltpu.VMEM((1, LANES), f32),
            pltpu.VMEM((rows * subs, 1, LANES), f32),
            pltpu.VMEM((slots, 2 * PAD, LANES), bf16),
            pltpu.VMEM((slots, 2 * PAD, LANES), bf16),
            pltpu.VMEM((slots, 2 * PAD, LANES), bf16),
            dma((5,)),
            dma((slots,)),
            dma((subs - 1,)),
            dma((subs - 1,)),
            dma((subs,)),
            dma,
            dma((ITERS,)),
            dma((ITERS,)),
            dma((ITERS,)),
            dma((ITERS,)),
            dma((mid,)),
            dma((mid,)),
            dma,
            dma,
        ],
        compiler_params=pltpu.CompilerParams(
            collective_id=0, has_side_effects=True, vmem_limit_bytes=40 * 1024 * 1024
        ),
    )(pin(blk_row), pin(blk_col), counts, pin(bias.reshape(own, LANES)), pin(mask.reshape(own, LANES)), pin(blocks))
    balanced, coverage = both[0], both[1]
    return balanced.reshape(-1), coverage.reshape(-1)


def solution(mesh):
    everywhere = P(("row", "sub"))
    return jax.shard_map(
        shards,
        mesh=mesh,
        in_specs=(P(("row", "sub"), None, None),) + (everywhere,) * 5,
        out_specs=(everywhere, everywhere),
        check_vma=False,
    )
```

```python
import functools

import jax
import jax.numpy as jnp
from jax import lax
from jax.experimental import pallas as pl
from jax.experimental.pallas import tpu as pltpu
from jax.sharding import PartitionSpec as P

BLK = 512
ITERS = 3
LANES = 128
PIECES = BLK // LANES
TILE = 8
PAD = 16
LEAD = TILE
LATE = 2


def kernel(
    row_hbm, col_hbm, count_hbm, bias_hbm, mask_hbm, blocks_ref, both_ref,
    row_ref, col_ref, count_ref, bias_ref, mask_ref, held, turned, weights, follow, part, edge_out, peers, before, after, last_peers, last_before, sums_out, sums_in, mask_a, mask_c, mask_r,
    small_sem, load_sem, gather_send, gather_recv, edge_send, edge_recv, peer_send, peer_recv,
    before_send, before_recv, after_send, after_recv, sums_send, sums_recv, known, ready,
):
    rows, subs = lax.axis_size("row"), lax.axis_size("sub")
    devices = rows * subs
    row, sub = lax.axis_index("row"), lax.axis_index("sub")
    slots = held.shape[0]
    own = bias_ref.shape[0]
    group = own * subs
    span = group + TILE
    has_before, has_after = row > 0, row < rows - 1

    def remote(src, dst, send, recv, target_row, target_sub):
        return pltpu.make_async_remote_copy(
            src_ref=src, dst_ref=dst, send_sem=send, recv_sem=recv,
            device_id=(target_row, target_sub), device_id_type=pl.DeviceIdType.MESH,
        )

    def wait_bytes(ref, sem):
        pltpu.make_async_copy(ref, ref, sem).wait()

    def ring(offset):
        return lax.rem(sub + offset, subs)

    loads = [pltpu.make_async_copy(blocks_ref.at[s], held.at[s], load_sem.at[s]) for s in range(slots)]
    smalls = [
        pltpu.make_async_copy(src, dst, small_sem.at[i])
        for i, (src, dst) in enumerate(
            ((bias_hbm, bias_ref), (mask_hbm, mask_ref), (row_hbm, row_ref), (col_hbm, col_ref), (count_hbm, count_ref))
        )
    ]
    barrier = pltpu.get_barrier_semaphore()

    def greet(target_row, target_sub, sem=barrier):
        pl.semaphore_signal(sem, inc=1, device_id=(target_row, target_sub), device_id_type=pl.DeviceIdType.MESH)

    for load in smalls:
        load.start()
    for offset in range(1, subs):
        greet(row, ring(offset))

    @pl.when(has_after)
    def _():
        for target in range(subs):
            greet(row + 1, target)

    for load in loads:
        load.start()

    stages = (rows - 1).bit_length()

    def tell(j):
        reach = 2**j

        @pl.when(row >= reach)
        def _():
            greet(row - reach, sub, known.at[j])

        @pl.when(row + reach < rows)
        def _():
            greet(row + reach, sub, known.at[j])

    def hear(j):
        reach = 2**j
        pl.semaphore_wait(known.at[j], jnp.where(row >= reach, 1, 0) + jnp.where(row + reach < rows, 1, 0))

    weights[0:LEAD, :] = jnp.zeros((LEAD, LANES), jnp.float32)
    rest = weights.shape[0] - LEAD - group
    weights[LEAD + group :, :] = jnp.zeros((rest, LANES), jnp.float32)

    @pl.when(jnp.logical_not(has_after))
    def _():
        follow[...] = jnp.zeros_like(follow)
        after[...] = jnp.zeros_like(after)

    @pl.when(jnp.logical_not(has_before))
    def _():
        before[...] = jnp.zeros_like(before)
        last_before[...] = jnp.zeros_like(last_before)

    @pl.when(jnp.logical_and(has_before, sub > 0))
    def _():
        last_before[...] = jnp.zeros_like(last_before)

    smalls[0].wait()
    smalls[1].wait()
    own_live = mask_ref[...].astype(jnp.float32)
    mine = pl.ds(pl.multiple_of(LEAD + sub * own, TILE), own)
    weights[mine, :] = bias_ref[...] * own_live

    pl.semaphore_wait(barrier, subs - 1 + jnp.where(has_before, subs, 0))

    for offset in range(1, subs):
        remote(
            weights.at[mine], weights.at[mine], gather_send.at[offset - 1], gather_recv.at[offset - 1], row, ring(offset)
        ).start()

    @pl.when(jnp.logical_and(has_before, sub == 0))
    def _():
        for target in range(subs):
            remote(
                weights.at[pl.ds(LEAD, TILE)], follow,
                edge_send.at[target], edge_recv, row - 1, target,
            ).start()

    @pl.when(has_before)
    def _():
        greet(row - 1, sub, ready)

    for load in smalls[2:]:
        load.wait()
    first_block = row * (group // PIECES)
    next_block = first_block + group // PIECES
    ids = lax.broadcasted_iota(jnp.int32, (PAD, LANES), 0)
    leaver = 0
    for s in range(slots):
        leaves = jnp.logical_and(s < count_ref[0], col_ref[s] == next_block)
        leaver = leaver + jnp.where(leaves, s, 0)
    order = [leaver] + [jnp.where(s >= leaver, s + 1, s) for s in range(slots - 1)]
    for s in range(slots):
        p = row_ref[order[s]] - first_block
        q = col_ref[order[s]] - first_block
        alive = jnp.where(order[s] < count_ref[0], 1.0, 0.0).astype(jnp.float32)
        same = jnp.where(p == q, 1.0, 0.0).astype(jnp.float32)
        at_p = jnp.where(ids == p, 1.0, 0.0).astype(jnp.float32)
        at_q = jnp.where(ids == q, 1.0, 0.0).astype(jnp.float32)
        for ref, value in (
            (mask_a, at_p * (0.5 * alive * same)),
            (mask_c, at_q * (alive * (1.0 - same))),
            (mask_r, at_p * (alive * (1.0 - same))),
        ):
            value = value.astype(jnp.bfloat16)
            ref[s] = jnp.concatenate([value, value], axis=0)

    for s in range(slots):
        loads[s].wait()
        turned[s] = held[s].T

    for offset in range(1, subs):
        theirs = weights.at[pl.ds(pl.multiple_of(LEAD + ring(subs - offset) * own, TILE), own)]
        wait_bytes(theirs, gather_recv.at[offset - 1])

    top = lax.broadcasted_iota(jnp.int32, (TILE, LANES), 0) < PIECES
    inner = weights[LEAD : LEAD + group, :]
    alive = inner > 0.0
    totals = []
    lane = lax.broadcasted_iota(jnp.int32, (1, LANES), 1)
    kept = jnp.sum(jnp.sum(own_live, axis=0, keepdims=True), axis=1, keepdims=True)

    def operand(start):
        value = jnp.concatenate(
            [weights[pl.ds(LEAD + start + q, PAD, stride=PIECES), :] for q in range(PIECES)], axis=1
        )
        high = value.astype(jnp.bfloat16)
        low = (value - high.astype(jnp.float32)).astype(jnp.bfloat16)
        return jnp.concatenate([high, low], axis=0)

    def wide(mask):
        return jnp.concatenate([mask] * PIECES, axis=1)

    def dot(left, right):
        return lax.dot_general(left, right, (((1,), (0,)), ((), ())), preferred_element_type=jnp.float32)

    edge_rows = pl.ds(group, TILE)
    edge_blocks = TILE // PIECES
    edge_at = group // PIECES
    last_slots = min(LATE, slots - 1)

    for k in range(ITERS):
        final = k == ITERS - 1
        here, lower, upper = operand(0), operand(-PIECES), operand(PIECES)
        first = dot(wide(mask_a[0]) * here + wide(mask_c[0]) * lower, held[order[0]])
        total = first
        for s in range(1, slots):
            if s == slots - last_slots:
                if k == 0:

                    @pl.when(has_after)
                    def _():
                        wait_bytes(follow, edge_recv)

                    back = jnp.where(top, follow[...], 0.0)
                    back_live = back > 0.0
                else:

                    @pl.when(has_after)
                    def _():
                        wait_bytes(after.at[k - 1], after_recv.at[k - 1])

                    back = jnp.where(back_live, 1.0 / (back_sums + jnp.sum(after[k - 1], axis=0)), 0.0)
                weights[LEAD + group : LEAD + span, :] = back
                whole = jnp.concatenate([inner, back], axis=0)
                upper_late = operand(PIECES)
            on = wide(mask_a[s]) * here
            total += dot(on + wide(mask_c[s]) * lower, held[order[s]])
            total += dot(on + wide(mask_r[s]) * upper, turned[order[s]])
            if s == 1:
                leaving = first[edge_at : edge_at + edge_blocks] + first[PAD + edge_at : PAD + edge_at + edge_blocks]
                for q in range(PIECES):
                    edge_out[k, pl.ds(q, edge_blocks, stride=PIECES), :] = leaving[:, q * LANES : (q + 1) * LANES]

                if k == 0:

                    @pl.when(has_after)
                    def _():
                        pl.semaphore_wait(ready, 1)

                    if stages:
                        tell(0)

                @pl.when(has_after)
                def _():
                    if final:
                        remote(
                            edge_out.at[k], last_before.at[sub], before_send.at[k], before_recv.at[k], row + 1, 0
                        ).start()
                    else:
                        for offset in range(subs):
                            remote(
                                edge_out.at[k], before.at[k, offset], before_send.at[k], before_recv.at[k],
                                row + 1, ring(offset),
                            ).start()

        total += dot(wide(mask_a[0]) * here + wide(mask_r[0]) * upper_late, turned[order[0]])
        total = total[:PAD] + total[PAD:]
        for q in range(PIECES):
            part[k, pl.ds(q, PAD, stride=PIECES), :] = total[:, q * LANES : (q + 1) * LANES]
        if not final:
            for offset in range(1, subs):
                remote(
                    part.at[k, pl.ds(0, span)], peers.at[k, offset - 1],
                    peer_send.at[k], peer_recv.at[k], row, ring(offset),
                ).start()

            @pl.when(has_before)
            def _():
                for offset in range(subs):
                    remote(
                        part.at[k, pl.ds(0, TILE)], after.at[k, offset], after_send.at[k], after_recv.at[k],
                        row - 1, ring(offset),
                    ).start()

            if k < stages:
                hear(k)
            if k + 1 < stages:
                tell(k + 1)
            product = whole * part[k, 0:span, :]
            totals.append(jnp.sum(jnp.sum(product, axis=0, keepdims=True), axis=1, keepdims=True))
            if k == 0:
                for offset in range(1, subs):
                    wait_bytes(weights.at[mine], gather_send.at[offset - 1])

                @pl.when(jnp.logical_and(has_before, sub == 0))
                def _():
                    for target in range(subs):
                        wait_bytes(weights.at[pl.ds(LEAD, TILE)], edge_send.at[target])

            @pl.when(has_before)
            def _():
                wait_bytes(before.at[k], before_recv.at[k])

            wait_bytes(peers.at[k], peer_recv.at[k])
            sums = part[k, 0:span, :]
            for offset in range(1, subs):
                sums += peers[k, offset - 1]
            front = sums[:TILE] + jnp.where(top, jnp.sum(before[k], axis=0), 0.0)
            back_sums = sums[group:]
            inner = jnp.where(alive, 1.0 / jnp.concatenate([front, sums[TILE:group]], axis=0), 0.0)
            weights[LEAD : LEAD + group, :] = inner
        else:
            for j in range(k, stages):
                hear(j)
                if j + 1 < stages:
                    tell(j + 1)
            product = whole * part[k, 0:span, :]
            last = jnp.sum(product, axis=0, keepdims=True)
            half = LANES // 2
            message = last + pltpu.roll(last, half, 1)
            for i, value in enumerate(totals + [kept]):
                message = jnp.where(lane == half + i, value, message)
            message = jnp.where(lane > half + ITERS - 1, 0.0, message)
            sums_out[...] = message

            @pl.loop(0, rows)
            def _(target_row):
                @pl.when(target_row != row)
                def _():
                    remote(sums_out, sums_in.at[row * subs], sums_send, sums_recv, target_row, sub).start()

                for offset in range(1, subs):
                    remote(
                        sums_out, sums_in.at[row * subs + offset], sums_send, sums_recv, target_row, ring(offset)
                    ).start()

            for offset in range(1, subs):
                theirs = pl.ds(pl.multiple_of(ring(offset) * own, TILE), own)
                remote(
                    part.at[k, theirs], last_peers.at[offset - 1], peer_send.at[k], peer_recv.at[k], row, ring(offset)
                ).start()

            wait_bytes(last_peers, peer_recv.at[k])

            @pl.when(jnp.logical_and(has_before, sub == 0))
            def _():
                wait_bytes(last_before, before_recv.at[k])

            sums = part[k, pl.ds(pl.multiple_of(sub * own, TILE), own), :] + jnp.sum(last_peers[...], axis=0)
            front = jnp.where(top, jnp.sum(last_before[...], axis=0), 0.0)
            if own > TILE:
                front = jnp.concatenate([front, jnp.zeros((own - TILE, LANES), jnp.float32)], axis=0)
            sums = sums + front
            now = weights[mine, :]
            inverse = jnp.where(own_live > 0.0, 1.0 / sums, 0.0)
            scaled = now * sums
            everyone = sums_in.at[pl.ds(0, devices - 1)]
            wait_bytes(everyone, sums_recv)
            sums_in[row * subs] = message
            grand = jnp.sum(sums_in[...], axis=0)
            half_sum = jnp.sum(jnp.where(lane < half, grand, 0.0), axis=1, keepdims=True)
            bins = grand[:, half + ITERS - 1 : half + ITERS]
            average = half_sum / bins
            scale = average
            for i in range(ITERS - 1):
                scale = scale * (grand[:, half + i : half + i + 1] / bins)
            both_ref[1] = scaled / average
            both_ref[0] = scale * inverse

    for k in range(ITERS):
        final = k == ITERS - 1
        wait_bytes(last_peers if final else peers.at[k], peer_send.at[k])

        @pl.when(has_after)
        def _():
            wait_bytes(last_before.at[0] if final else before.at[k], before_send.at[k])

        if not final:

            @pl.when(has_before)
            def _():
                wait_bytes(after.at[k], after_send.at[k])

    wait_bytes(sums_in.at[pl.ds(0, devices - 1)], sums_send)


def shards(blocks, blk_row, blk_col, counts, bias, mask):
    rows, subs = lax.axis_size("row"), lax.axis_size("sub")
    slots = blocks.shape[0]
    own = bias.shape[0] // LANES
    group = own * subs
    span = group + TILE
    mid = ITERS - 1
    f32, bf16 = jnp.float32, jnp.bfloat16
    dma = pltpu.SemaphoreType.DMA
    vmem = pl.BlockSpec(memory_space=pltpu.VMEM)
    def pin(x):
        return pltpu.with_memory_space_constraint(x, pltpu.HBM)

    both = pl.pallas_call(
        kernel,
        out_shape=pltpu.VMEM((2, own, LANES), f32),
        in_specs=[pl.BlockSpec(memory_space=pltpu.HBM)] * 6,
        out_specs=vmem,
        scratch_shapes=[
            pltpu.SMEM((slots,), jnp.int32),
            pltpu.SMEM((slots,), jnp.int32),
            pltpu.SMEM((1,), jnp.int32),
            pltpu.VMEM((own, LANES), f32),
            pltpu.VMEM((own, LANES), jnp.int32),
            pltpu.VMEM(blocks.shape, bf16),
            pltpu.VMEM(blocks.shape, bf16),
            pltpu.VMEM((LEAD + PAD * PIECES + TILE, LANES), f32),
            pltpu.VMEM((TILE, LANES), f32),
            pltpu.VMEM((ITERS, PAD * PIECES, LANES), f32),
            pltpu.VMEM((ITERS, TILE, LANES), f32),
            pltpu.VMEM((mid, subs - 1, span, LANES), f32),
            pltpu.VMEM((mid, subs, TILE, LANES), f32),
            pltpu.VMEM((mid, subs, TILE, LANES), f32),
            pltpu.VMEM((subs - 1, own, LANES), f32),
            pltpu.VMEM((subs, TILE, LANES), f32),
            pltpu.VMEM((1, LANES), f32),
            pltpu.VMEM((rows * subs, 1, LANES), f32),
            pltpu.VMEM((slots, 2 * PAD, LANES), bf16),
            pltpu.VMEM((slots, 2 * PAD, LANES), bf16),
            pltpu.VMEM((slots, 2 * PAD, LANES), bf16),
            dma((5,)),
            dma((slots,)),
            dma((subs - 1,)),
            dma((subs - 1,)),
            dma((subs,)),
            dma,
            dma((ITERS,)),
            dma((ITERS,)),
            dma((ITERS,)),
            dma((ITERS,)),
            dma((mid,)),
            dma((mid,)),
            dma,
            dma,
            pltpu.SemaphoreType.REGULAR((max((rows - 1).bit_length(), 1),)),
            pltpu.SemaphoreType.REGULAR,
        ],
        compiler_params=pltpu.CompilerParams(
            collective_id=0, has_side_effects=True, vmem_limit_bytes=40 * 1024 * 1024
        ),
    )(pin(blk_row), pin(blk_col), counts, pin(bias.reshape(own, LANES)), pin(mask.reshape(own, LANES)), pin(blocks))
    balanced, coverage = both[0], both[1]
    return balanced.reshape(-1), coverage.reshape(-1)


def solution(mesh):
    everywhere = P(("row", "sub"))
    return jax.shard_map(
        shards,
        mesh=mesh,
        in_specs=(P(("row", "sub"), None, None),) + (everywhere,) * 5,
        out_specs=(everywhere, everywhere),
        check_vma=False,
    )
```

```python
import functools

import jax
import jax.numpy as jnp
from jax import lax
from jax.experimental import pallas as pl
from jax.experimental.pallas import tpu as pltpu
from jax.sharding import PartitionSpec as P

BLK = 512
ITERS = 3
LANES = 128
PIECES = BLK // LANES
TILE = 8
PAD = 8
LEAD = TILE
LATE = 2


def kernel(
    row_hbm, col_hbm, count_hbm, bias_hbm, mask_hbm, blocks_ref, both_ref,
    row_ref, col_ref, count_ref, bias_ref, mask_ref, held, turned, weights, follow, part, peers, before, after, last_peers, last_before, sums_out, sums_in, mask_a, mask_c, mask_r, mask_e,
    small_sem, load_sem, gather_send, gather_recv, edge_send, edge_recv, peer_send, peer_recv,
    before_send, before_recv, after_send, after_recv, sums_send, sums_recv, known, ready,
):
    rows, subs = lax.axis_size("row"), lax.axis_size("sub")
    devices = rows * subs
    row, sub = lax.axis_index("row"), lax.axis_index("sub")
    slots = held.shape[0]
    own = bias_ref.shape[0]
    group = own * subs
    span = group + TILE
    has_before, has_after = row > 0, row < rows - 1

    def remote(src, dst, send, recv, target_row, target_sub):
        return pltpu.make_async_remote_copy(
            src_ref=src, dst_ref=dst, send_sem=send, recv_sem=recv,
            device_id=(target_row, target_sub), device_id_type=pl.DeviceIdType.MESH,
        )

    def wait_bytes(ref, sem):
        pltpu.make_async_copy(ref, ref, sem).wait()

    def ring(offset):
        return lax.rem(sub + offset, subs)

    others = sorted(range(1, subs), key=lambda offset: -min(offset, subs - offset))
    loads = [pltpu.make_async_copy(blocks_ref.at[s], held.at[s], load_sem.at[s]) for s in range(slots)]
    smalls = [
        pltpu.make_async_copy(src, dst, small_sem.at[i])
        for i, (src, dst) in enumerate(
            ((bias_hbm, bias_ref), (mask_hbm, mask_ref), (row_hbm, row_ref), (col_hbm, col_ref), (count_hbm, count_ref))
        )
    ]
    barrier = pltpu.get_barrier_semaphore()

    def greet(target_row, target_sub, sem=barrier):
        pl.semaphore_signal(sem, inc=1, device_id=(target_row, target_sub), device_id_type=pl.DeviceIdType.MESH)

    for offset in others:
        greet(row, ring(offset))
    for load in smalls:
        load.start()

    @pl.when(has_after)
    def _():
        for target in range(subs):
            greet(row + 1, target)

    for load in loads:
        load.start()

    stages = (rows - 1).bit_length()

    def tell(j):
        reach = 2**j

        @pl.when(row >= reach)
        def _():
            greet(row - reach, sub, known.at[j])

        @pl.when(row + reach < rows)
        def _():
            greet(row + reach, sub, known.at[j])

    def hear(j):
        reach = 2**j
        pl.semaphore_wait(known.at[j], jnp.where(row >= reach, 1, 0) + jnp.where(row + reach < rows, 1, 0))

    weights[0:LEAD, :] = jnp.zeros((LEAD, LANES), jnp.float32)
    rest = weights.shape[0] - LEAD - group
    weights[LEAD + group :, :] = jnp.zeros((rest, LANES), jnp.float32)
    for k in range(ITERS):
        part[k, group:span, :] = jnp.zeros((TILE, LANES), jnp.float32)

    @pl.when(jnp.logical_not(has_after))
    def _():
        follow[...] = jnp.zeros_like(follow)
        after[...] = jnp.zeros_like(after)

    @pl.when(jnp.logical_not(has_before))
    def _():
        before[...] = jnp.zeros_like(before)
        last_before[...] = jnp.zeros_like(last_before)

    @pl.when(jnp.logical_and(has_before, sub > 0))
    def _():
        last_before[...] = jnp.zeros_like(last_before)

    smalls[0].wait()
    smalls[1].wait()
    own_live = mask_ref[...].astype(jnp.float32)
    mine = pl.ds(pl.multiple_of(LEAD + sub * own, TILE), own)
    weights[mine, :] = bias_ref[...] * own_live

    pl.semaphore_wait(barrier, subs - 1 + jnp.where(has_before, subs, 0))

    for offset in others:
        remote(
            weights.at[mine], weights.at[mine], gather_send.at[offset - 1], gather_recv.at[offset - 1], row, ring(offset)
        ).start()

    @pl.when(jnp.logical_and(has_before, sub == 0))
    def _():
        for target in range(subs):
            remote(
                weights.at[pl.ds(LEAD, TILE)], follow,
                edge_send.at[target], edge_recv, row - 1, target,
            ).start()

    @pl.when(has_before)
    def _():
        greet(row - 1, sub, ready)

    for load in smalls[2:]:
        load.wait()
    first_block = row * (group // PIECES)
    next_block = first_block + group // PIECES
    ids = lax.broadcasted_iota(jnp.int32, (PAD, LANES), 0)
    leaver, leaving = 0, 0.0
    for s in range(slots):
        leaves = jnp.logical_and(s < count_ref[0], col_ref[s] == next_block)
        leaver = leaver + jnp.where(leaves, s, 0)
        leaving = leaving + jnp.where(leaves, 1.0, 0.0).astype(jnp.float32)
    order = [leaver] + [jnp.where(s >= leaver, s + 1, s) for s in range(slots - 1)]
    for s in range(slots):
        p = row_ref[order[s]] - first_block
        q = col_ref[order[s]] - first_block
        alive = jnp.where(order[s] < count_ref[0], 1.0, 0.0).astype(jnp.float32)
        same = jnp.where(p == q, 1.0, 0.0).astype(jnp.float32)
        at_p = jnp.where(ids == p, 1.0, 0.0).astype(jnp.float32)
        at_q = jnp.where(ids == q, 1.0, 0.0).astype(jnp.float32)
        for ref, value in (
            (mask_a, at_p * (0.5 * alive * same)),
            (mask_c, at_q * (alive * (1.0 - same))),
            (mask_r, at_p * (alive * (1.0 - same))),
        ):
            value = value.astype(jnp.bfloat16)
            ref[s] = jnp.concatenate([value, value], axis=0)
    value = (jnp.where(ids == group // PIECES - 1, 1.0, 0.0).astype(jnp.float32) * leaving).astype(jnp.bfloat16)
    mask_e[...] = jnp.concatenate([value, value], axis=0)

    for s in range(slots):
        loads[s].wait()
        turned[s] = held[s].T

    for offset in range(1, subs):
        theirs = weights.at[pl.ds(pl.multiple_of(LEAD + ring(subs - offset) * own, TILE), own)]
        wait_bytes(theirs, gather_recv.at[offset - 1])

    top = lax.broadcasted_iota(jnp.int32, (TILE, LANES), 0) < PIECES
    inner = weights[LEAD : LEAD + group, :]
    alive = inner > 0.0
    totals = []
    lane = lax.broadcasted_iota(jnp.int32, (1, LANES), 1)
    kept = jnp.sum(jnp.sum(own_live, axis=0, keepdims=True), axis=1, keepdims=True)

    def operand(start):
        value = jnp.concatenate(
            [weights[pl.ds(LEAD + start + q, PAD, stride=PIECES), :] for q in range(PIECES)], axis=1
        )
        high = value.astype(jnp.bfloat16)
        low = (value - high.astype(jnp.float32)).astype(jnp.bfloat16)
        return jnp.concatenate([high, low], axis=0)

    def wide(mask):
        return jnp.concatenate([mask] * PIECES, axis=1)

    def dot(left, right):
        return lax.dot_general(left, right, (((1,), (0,)), ((), ())), preferred_element_type=jnp.float32)

    edge_rows = pl.ds(group, TILE)
    last_slots = min(LATE, slots - 1)

    for k in range(ITERS):
        final = k == ITERS - 1
        here, lower, upper = operand(0), operand(-PIECES), operand(PIECES)
        first = dot(wide(mask_a[0] + mask_e[...]) * here + wide(mask_c[0]) * lower, held[order[0]])
        total = first * (1.0 - leaving)
        for s in range(1, slots):
            if s == slots - last_slots:
                if k == 0:

                    @pl.when(has_after)
                    def _():
                        wait_bytes(follow, edge_recv)

                    back = jnp.where(top, follow[...], 0.0)
                    back_live = back > 0.0
                else:

                    @pl.when(has_after)
                    def _():
                        wait_bytes(after.at[k - 1], after_recv.at[k - 1])

                    back = jnp.where(back_live, 1.0 / (back_sums + jnp.sum(after[k - 1], axis=0)), 0.0)
                weights[LEAD + group : LEAD + span, :] = back
                whole = jnp.concatenate([inner, back], axis=0)
                upper_late = operand(PIECES)
            on = wide(mask_a[s]) * here
            total += dot(on + wide(mask_c[s]) * lower, held[order[s]])
            total += dot(on + wide(mask_r[s]) * upper, turned[order[s]])
            if s == 1:
                out = (first[PAD - 1 : PAD] + first[2 * PAD - 1 : 2 * PAD]) * leaving
                for q in range(PIECES):
                    part[k, group + q : group + q + 1, :] = out[:, q * LANES : (q + 1) * LANES]

                if k == 0:

                    @pl.when(has_after)
                    def _():
                        pl.semaphore_wait(ready, 1)

                    if stages:
                        tell(0)

                @pl.when(has_after)
                def _():
                    if final:
                        remote(
                            part.at[k, edge_rows], last_before.at[sub], before_send.at[k], before_recv.at[k], row + 1, 0
                        ).start()
                    else:
                        for offset in range(subs):
                            remote(
                                part.at[k, edge_rows], before.at[k, offset], before_send.at[k], before_recv.at[k],
                                row + 1, ring(offset),
                            ).start()

        total += dot(wide(mask_a[0]) * here + wide(mask_r[0]) * upper_late, turned[order[0]])
        total = total[:PAD] + total[PAD:]
        for q in range(PIECES):
            part[k, pl.ds(q, PAD, stride=PIECES), :] = total[:, q * LANES : (q + 1) * LANES]
        if not final:
            for offset in others:
                remote(
                    part.at[k, pl.ds(0, span)], peers.at[k, offset - 1],
                    peer_send.at[k], peer_recv.at[k], row, ring(offset),
                ).start()

            @pl.when(has_before)
            def _():
                for offset in range(subs):
                    remote(
                        part.at[k, pl.ds(0, TILE)], after.at[k, offset], after_send.at[k], after_recv.at[k],
                        row - 1, ring(offset),
                    ).start()

            if k < stages:
                hear(k)
            if k + 1 < stages:
                tell(k + 1)
            product = whole * part[k, 0:span, :]
            totals.append(jnp.sum(jnp.sum(product, axis=0, keepdims=True), axis=1, keepdims=True))
            if k == 0:
                for offset in range(1, subs):
                    wait_bytes(weights.at[mine], gather_send.at[offset - 1])

                @pl.when(jnp.logical_and(has_before, sub == 0))
                def _():
                    for target in range(subs):
                        wait_bytes(weights.at[pl.ds(LEAD, TILE)], edge_send.at[target])

            @pl.when(has_before)
            def _():
                wait_bytes(before.at[k], before_recv.at[k])

            wait_bytes(peers.at[k], peer_recv.at[k])
            sums = part[k, 0:span, :]
            for offset in range(1, subs):
                sums += peers[k, offset - 1]
            front = sums[:TILE] + jnp.where(top, jnp.sum(before[k], axis=0), 0.0)
            back_sums = sums[group:]
            inner = jnp.where(alive, 1.0 / jnp.concatenate([front, sums[TILE:group]], axis=0), 0.0)
            weights[LEAD : LEAD + group, :] = inner
        else:
            scalars = jnp.zeros((1, LANES), jnp.float32)
            for i, value in enumerate(totals + [kept]):
                scalars = jnp.where(lane == i, value, scalars)
            sums_out[1:2, :] = scalars
            for j in range(k, stages):
                hear(j)
                if j + 1 < stages:
                    tell(j + 1)
            product = whole * part[k, 0:span, :]
            sums_out[0:1, :] = jnp.sum(product, axis=0, keepdims=True)

            @pl.loop(0, rows)
            def _(target_row):
                @pl.when(target_row != row)
                def _():
                    remote(sums_out, sums_in.at[row * subs], sums_send, sums_recv, target_row, sub).start()

                for offset in range(1, subs):
                    remote(
                        sums_out, sums_in.at[row * subs + offset], sums_send, sums_recv, target_row, ring(offset)
                    ).start()

            for offset in others:
                theirs = pl.ds(pl.multiple_of(ring(offset) * own, TILE), own)
                remote(
                    part.at[k, theirs], last_peers.at[offset - 1], peer_send.at[k], peer_recv.at[k], row, ring(offset)
                ).start()

            wait_bytes(last_peers, peer_recv.at[k])

            @pl.when(jnp.logical_and(has_before, sub == 0))
            def _():
                wait_bytes(last_before, before_recv.at[k])

            sums = part[k, pl.ds(pl.multiple_of(sub * own, TILE), own), :] + jnp.sum(last_peers[...], axis=0)
            front = jnp.where(top, jnp.sum(last_before[...], axis=0), 0.0)
            if own > TILE:
                front = jnp.concatenate([front, jnp.zeros((own - TILE, LANES), jnp.float32)], axis=0)
            sums = sums + front
            now = weights[mine, :]
            inverse = jnp.where(own_live > 0.0, 1.0 / sums, 0.0)
            scaled = now * sums
            everyone = sums_in.at[pl.ds(0, devices - 1)]
            wait_bytes(everyone, sums_recv)
            sums_in[row * subs] = sums_out[...]
            grand = jnp.sum(sums_in[...], axis=0)
            bins = grand[1:2, ITERS - 1 : ITERS]
            average = jnp.sum(grand[0:1], axis=1, keepdims=True) / bins
            scale = average
            for i in range(ITERS - 1):
                scale = scale * (grand[1:2, i : i + 1] / bins)
            both_ref[1] = scaled / average
            both_ref[0] = scale * inverse

    for k in range(ITERS):
        final = k == ITERS - 1
        wait_bytes(last_peers if final else peers.at[k], peer_send.at[k])

        @pl.when(has_after)
        def _():
            wait_bytes(last_before.at[0] if final else before.at[k], before_send.at[k])

        if not final:

            @pl.when(has_before)
            def _():
                wait_bytes(after.at[k], after_send.at[k])

    wait_bytes(sums_in.at[pl.ds(0, devices - 1)], sums_send)


def shards(blocks, blk_row, blk_col, counts, bias, mask):
    rows, subs = lax.axis_size("row"), lax.axis_size("sub")
    slots = blocks.shape[0]
    own = bias.shape[0] // LANES
    group = own * subs
    span = group + TILE
    mid = ITERS - 1
    f32, bf16 = jnp.float32, jnp.bfloat16
    dma = pltpu.SemaphoreType.DMA
    vmem = pl.BlockSpec(memory_space=pltpu.VMEM)
    def pin(x):
        return pltpu.with_memory_space_constraint(x, pltpu.HBM)

    both = pl.pallas_call(
        kernel,
        out_shape=pltpu.VMEM((2, own, LANES), f32),
        in_specs=[pl.BlockSpec(memory_space=pltpu.HBM)] * 6,
        out_specs=vmem,
        scratch_shapes=[
            pltpu.SMEM((slots,), jnp.int32),
            pltpu.SMEM((slots,), jnp.int32),
            pltpu.SMEM((1,), jnp.int32),
            pltpu.VMEM((own, LANES), f32),
            pltpu.VMEM((own, LANES), jnp.int32),
            pltpu.VMEM(blocks.shape, bf16),
            pltpu.VMEM(blocks.shape, bf16),
            pltpu.VMEM((LEAD + PAD * PIECES + TILE, LANES), f32),
            pltpu.VMEM((TILE, LANES), f32),
            pltpu.VMEM((ITERS, span, LANES), f32),
            pltpu.VMEM((mid, subs - 1, span, LANES), f32),
            pltpu.VMEM((mid, subs, TILE, LANES), f32),
            pltpu.VMEM((mid, subs, TILE, LANES), f32),
            pltpu.VMEM((subs - 1, own, LANES), f32),
            pltpu.VMEM((subs, TILE, LANES), f32),
            pltpu.VMEM((2, LANES), f32),
            pltpu.VMEM((rows * subs, 2, LANES), f32),
            pltpu.VMEM((slots, 2 * PAD, LANES), bf16),
            pltpu.VMEM((slots, 2 * PAD, LANES), bf16),
            pltpu.VMEM((slots, 2 * PAD, LANES), bf16),
            pltpu.VMEM((2 * PAD, LANES), bf16),
            dma((5,)),
            dma((slots,)),
            dma((subs - 1,)),
            dma((subs - 1,)),
            dma((subs,)),
            dma,
            dma((ITERS,)),
            dma((ITERS,)),
            dma((ITERS,)),
            dma((ITERS,)),
            dma((mid,)),
            dma((mid,)),
            dma,
            dma,
            pltpu.SemaphoreType.REGULAR((max((rows - 1).bit_length(), 1),)),
            pltpu.SemaphoreType.REGULAR,
        ],
        compiler_params=pltpu.CompilerParams(
            collective_id=0, has_side_effects=True, vmem_limit_bytes=40 * 1024 * 1024
        ),
    )(pin(blk_row), pin(blk_col), counts, pin(bias.reshape(own, LANES)), pin(mask.reshape(own, LANES)), pin(blocks))
    balanced, coverage = both[0], both[1]
    return balanced.reshape(-1), coverage.reshape(-1)


def solution(mesh):
    everywhere = P(("row", "sub"))
    return jax.shard_map(
        shards,
        mesh=mesh,
        in_specs=(P(("row", "sub"), None, None),) + (everywhere,) * 5,
        out_specs=(everywhere, everywhere),
        check_vma=False,
    )
```

```python
import functools

import jax
import jax.numpy as jnp
from jax import lax
from jax.experimental import pallas as pl
from jax.experimental.pallas import tpu as pltpu
from jax.sharding import PartitionSpec as P

BLK = 512
ITERS = 3
LANES = 128
PIECES = BLK // LANES
TILE = 8
PAD = 8
LEAD = TILE
LATE = 2
LINK = 1


def kernel(
    row_hbm, col_hbm, count_hbm, bias_hbm, mask_hbm, blocks_ref, both_ref,
    row_ref, col_ref, count_ref, bias_ref, mask_ref, held, turned, weights, follow, part, peers, before, after, last_peers, last_before, sums_out, sums_in, mask_a, mask_c, mask_r, mask_e,
    small_sem, load_sem, gather_send, gather_recv, edge_send, edge_recv, peer_send, peer_recv,
    before_send, before_recv, after_send, after_recv, sums_send, sums_recv, known, ready,
):
    rows, subs = lax.axis_size("row"), lax.axis_size("sub")
    devices = rows * subs
    row, sub = lax.axis_index("row"), lax.axis_index("sub")
    slots = held.shape[0]
    own = bias_ref.shape[0]
    group = own * subs
    span = group + TILE
    has_before, has_after = row > 0, row < rows - 1

    def remote(src, dst, send, recv, target_row, target_sub):
        return pltpu.make_async_remote_copy(
            src_ref=src, dst_ref=dst, send_sem=send, recv_sem=recv,
            device_id=(target_row, target_sub), device_id_type=pl.DeviceIdType.MESH,
        )

    def wait_bytes(ref, sem):
        pltpu.make_async_copy(ref, ref, sem).wait()

    def ring(offset):
        return lax.rem(sub + offset, subs)

    others = sorted(range(1, subs), key=lambda offset: -min(offset, subs - offset))
    loads = [pltpu.make_async_copy(blocks_ref.at[s], held.at[s], load_sem.at[s]) for s in range(slots)]
    smalls = [
        pltpu.make_async_copy(src, dst, small_sem.at[i])
        for i, (src, dst) in enumerate(
            ((bias_hbm, bias_ref), (mask_hbm, mask_ref), (row_hbm, row_ref), (col_hbm, col_ref), (count_hbm, count_ref))
        )
    ]
    barrier = pltpu.get_barrier_semaphore()

    def greet(target_row, target_sub, sem=barrier):
        pl.semaphore_signal(sem, inc=1, device_id=(target_row, target_sub), device_id_type=pl.DeviceIdType.MESH)

    for offset in others:
        greet(row, ring(offset))
    for load in smalls:
        load.start()

    @pl.when(has_after)
    def _():
        greet(row + 1, LINK)

    for load in loads:
        load.start()

    stages = (rows - 1).bit_length()

    def tell(j):
        reach = 2**j

        @pl.when(row >= reach)
        def _():
            greet(row - reach, sub, known.at[j])

        @pl.when(row + reach < rows)
        def _():
            greet(row + reach, sub, known.at[j])

    def hear(j):
        reach = 2**j
        pl.semaphore_wait(known.at[j], jnp.where(row >= reach, 1, 0) + jnp.where(row + reach < rows, 1, 0))

    weights[0:LEAD, :] = jnp.zeros((LEAD, LANES), jnp.float32)
    rest = weights.shape[0] - LEAD - group
    weights[LEAD + group :, :] = jnp.zeros((rest, LANES), jnp.float32)
    for k in range(ITERS):
        part[k, group:span, :] = jnp.zeros((TILE, LANES), jnp.float32)

    @pl.when(jnp.logical_not(has_after))
    def _():
        follow[...] = jnp.zeros_like(follow)
        after[...] = jnp.zeros_like(after)

    @pl.when(jnp.logical_not(has_before))
    def _():
        before[...] = jnp.zeros_like(before)
        last_before[...] = jnp.zeros_like(last_before)

    @pl.when(jnp.logical_and(has_before, sub > 0))
    def _():
        last_before[...] = jnp.zeros_like(last_before)

    smalls[0].wait()
    smalls[1].wait()
    own_live = mask_ref[...].astype(jnp.float32)
    mine = pl.ds(pl.multiple_of(LEAD + sub * own, TILE), own)
    weights[mine, :] = bias_ref[...] * own_live

    linked = jnp.logical_and(has_before, sub == LINK)
    pl.semaphore_wait(barrier, subs - 1 + jnp.where(linked, subs, 0))

    for offset in others:
        remote(
            weights.at[mine], weights.at[mine], gather_send.at[offset - 1], gather_recv.at[offset - 1], row, ring(offset)
        ).start()

    @pl.when(linked)
    def _():
        for target in range(subs):
            greet(row - 1, target, ready)

    for load in smalls[2:]:
        load.wait()
    first_block = row * (group // PIECES)
    next_block = first_block + group // PIECES
    ids = lax.broadcasted_iota(jnp.int32, (PAD, LANES), 0)
    leaver, leaving = 0, 0.0
    for s in range(slots):
        leaves = jnp.logical_and(s < count_ref[0], col_ref[s] == next_block)
        leaver = leaver + jnp.where(leaves, s, 0)
        leaving = leaving + jnp.where(leaves, 1.0, 0.0).astype(jnp.float32)
    order = [leaver] + [jnp.where(s >= leaver, s + 1, s) for s in range(slots - 1)]
    for s in range(slots):
        p = row_ref[order[s]] - first_block
        q = col_ref[order[s]] - first_block
        alive = jnp.where(order[s] < count_ref[0], 1.0, 0.0).astype(jnp.float32)
        same = jnp.where(p == q, 1.0, 0.0).astype(jnp.float32)
        at_p = jnp.where(ids == p, 1.0, 0.0).astype(jnp.float32)
        at_q = jnp.where(ids == q, 1.0, 0.0).astype(jnp.float32)
        for ref, value in (
            (mask_a, at_p * (0.5 * alive * same)),
            (mask_c, at_q * (alive * (1.0 - same))),
            (mask_r, at_p * (alive * (1.0 - same))),
        ):
            value = value.astype(jnp.bfloat16)
            ref[s] = jnp.concatenate([value, value], axis=0)
    value = (jnp.where(ids == group // PIECES - 1, 1.0, 0.0).astype(jnp.float32) * leaving).astype(jnp.bfloat16)
    mask_e[...] = jnp.concatenate([value, value], axis=0)

    first_own = weights.at[pl.ds(LEAD, own)]

    @pl.when(linked)
    def _():
        wait_bytes(first_own, gather_recv.at[LINK - 1])
        for target in range(subs):
            remote(
                weights.at[pl.ds(LEAD, TILE)], follow,
                edge_send.at[target], edge_recv, row - 1, target,
            ).start()

    for s in range(slots):
        loads[s].wait()
        turned[s] = held[s].T

    for offset in range(1, subs):
        theirs = weights.at[pl.ds(pl.multiple_of(LEAD + ring(subs - offset) * own, TILE), own)]
        if offset == LINK:

            @pl.when(jnp.logical_not(linked))
            def _():
                wait_bytes(theirs, gather_recv.at[offset - 1])
        else:
            wait_bytes(theirs, gather_recv.at[offset - 1])

    top = lax.broadcasted_iota(jnp.int32, (TILE, LANES), 0) < PIECES
    inner = weights[LEAD : LEAD + group, :]
    alive = inner > 0.0
    totals = []
    lane = lax.broadcasted_iota(jnp.int32, (1, LANES), 1)
    kept = jnp.sum(jnp.sum(own_live, axis=0, keepdims=True), axis=1, keepdims=True)

    def operand(start):
        value = jnp.concatenate(
            [weights[pl.ds(LEAD + start + q, PAD, stride=PIECES), :] for q in range(PIECES)], axis=1
        )
        high = value.astype(jnp.bfloat16)
        low = (value - high.astype(jnp.float32)).astype(jnp.bfloat16)
        return jnp.concatenate([high, low], axis=0)

    def wide(mask):
        return jnp.concatenate([mask] * PIECES, axis=1)

    def dot(left, right):
        return lax.dot_general(left, right, (((1,), (0,)), ((), ())), preferred_element_type=jnp.float32)

    edge_rows = pl.ds(group, TILE)
    last_slots = min(LATE, slots - 1)

    for k in range(ITERS):
        final = k == ITERS - 1
        here, lower, upper = operand(0), operand(-PIECES), operand(PIECES)
        first = dot(wide(mask_a[0] + mask_e[...]) * here + wide(mask_c[0]) * lower, held[order[0]])
        total = first * (1.0 - leaving)
        for s in range(1, slots):
            if s == slots - last_slots:
                if k == 0:

                    @pl.when(has_after)
                    def _():
                        wait_bytes(follow, edge_recv)

                    back = jnp.where(top, follow[...], 0.0)
                    back_live = back > 0.0
                else:

                    @pl.when(has_after)
                    def _():
                        wait_bytes(after.at[k - 1], after_recv.at[k - 1])

                    back = jnp.where(back_live, 1.0 / (back_sums + jnp.sum(after[k - 1], axis=0)), 0.0)
                weights[LEAD + group : LEAD + span, :] = back
                whole = jnp.concatenate([inner, back], axis=0)
                upper_late = operand(PIECES)
            on = wide(mask_a[s]) * here
            total += dot(on + wide(mask_c[s]) * lower, held[order[s]])
            total += dot(on + wide(mask_r[s]) * upper, turned[order[s]])
            if s == 1:
                out = (first[PAD - 1 : PAD] + first[2 * PAD - 1 : 2 * PAD]) * leaving
                for q in range(PIECES):
                    part[k, group + q : group + q + 1, :] = out[:, q * LANES : (q + 1) * LANES]

                if k == 0:

                    @pl.when(has_after)
                    def _():
                        pl.semaphore_wait(ready, 1)

                    if stages:
                        tell(0)

                @pl.when(has_after)
                def _():
                    if final:
                        remote(
                            part.at[k, edge_rows], last_before.at[sub], before_send.at[k], before_recv.at[k], row + 1, 0
                        ).start()
                    else:
                        for offset in range(subs):
                            remote(
                                part.at[k, edge_rows], before.at[k, offset], before_send.at[k], before_recv.at[k],
                                row + 1, ring(offset),
                            ).start()

        total += dot(wide(mask_a[0]) * here + wide(mask_r[0]) * upper_late, turned[order[0]])
        total = total[:PAD] + total[PAD:]
        for q in range(PIECES):
            part[k, pl.ds(q, PAD, stride=PIECES), :] = total[:, q * LANES : (q + 1) * LANES]
        if not final:
            for offset in others:
                remote(
                    part.at[k, pl.ds(0, span)], peers.at[k, offset - 1],
                    peer_send.at[k], peer_recv.at[k], row, ring(offset),
                ).start()

            @pl.when(has_before)
            def _():
                for offset in range(subs):
                    remote(
                        part.at[k, pl.ds(0, TILE)], after.at[k, offset], after_send.at[k], after_recv.at[k],
                        row - 1, ring(offset),
                    ).start()

            if k < stages:
                hear(k)
            if k + 1 < stages:
                tell(k + 1)
            product = whole * part[k, 0:span, :]
            totals.append(jnp.sum(jnp.sum(product, axis=0, keepdims=True), axis=1, keepdims=True))
            if k == 0:
                for offset in range(1, subs):
                    wait_bytes(weights.at[mine], gather_send.at[offset - 1])

                @pl.when(linked)
                def _():
                    for target in range(subs):
                        wait_bytes(weights.at[pl.ds(LEAD, TILE)], edge_send.at[target])

            @pl.when(has_before)
            def _():
                wait_bytes(before.at[k], before_recv.at[k])

            wait_bytes(peers.at[k], peer_recv.at[k])
            sums = part[k, 0:span, :]
            for offset in range(1, subs):
                sums += peers[k, offset - 1]
            front = sums[:TILE] + jnp.where(top, jnp.sum(before[k], axis=0), 0.0)
            back_sums = sums[group:]
            inner = jnp.where(alive, 1.0 / jnp.concatenate([front, sums[TILE:group]], axis=0), 0.0)
            weights[LEAD : LEAD + group, :] = inner
        else:
            scalars = jnp.zeros((1, LANES), jnp.float32)
            for i, value in enumerate(totals + [kept]):
                scalars = jnp.where(lane == i, value, scalars)
            sums_out[1:2, :] = scalars
            for j in range(k, stages):
                hear(j)
                if j + 1 < stages:
                    tell(j + 1)
            product = whole * part[k, 0:span, :]
            sums_out[0:1, :] = jnp.sum(product, axis=0, keepdims=True)

            @pl.loop(0, rows)
            def _(target_row):
                @pl.when(target_row != row)
                def _():
                    remote(sums_out, sums_in.at[row * subs], sums_send, sums_recv, target_row, sub).start()

                for offset in range(1, subs):
                    remote(
                        sums_out, sums_in.at[row * subs + offset], sums_send, sums_recv, target_row, ring(offset)
                    ).start()

            for offset in others:
                theirs = pl.ds(pl.multiple_of(ring(offset) * own, TILE), own)
                remote(
                    part.at[k, theirs], last_peers.at[offset - 1], peer_send.at[k], peer_recv.at[k], row, ring(offset)
                ).start()

            wait_bytes(last_peers, peer_recv.at[k])

            @pl.when(jnp.logical_and(has_before, sub == 0))
            def _():
                wait_bytes(last_before, before_recv.at[k])

            sums = part[k, pl.ds(pl.multiple_of(sub * own, TILE), own), :] + jnp.sum(last_peers[...], axis=0)
            front = jnp.where(top, jnp.sum(last_before[...], axis=0), 0.0)
            if own > TILE:
                front = jnp.concatenate([front, jnp.zeros((own - TILE, LANES), jnp.float32)], axis=0)
            sums = sums + front
            now = weights[mine, :]
            inverse = jnp.where(own_live > 0.0, 1.0 / sums, 0.0)
            scaled = now * sums
            everyone = sums_in.at[pl.ds(0, devices - 1)]
            wait_bytes(everyone, sums_recv)
            sums_in[row * subs] = sums_out[...]
            grand = jnp.sum(sums_in[...], axis=0)
            bins = grand[1:2, ITERS - 1 : ITERS]
            average = jnp.sum(grand[0:1], axis=1, keepdims=True) / bins
            scale = average
            for i in range(ITERS - 1):
                scale = scale * (grand[1:2, i : i + 1] / bins)
            both_ref[1] = scaled / average
            both_ref[0] = scale * inverse

    for k in range(ITERS):
        final = k == ITERS - 1
        wait_bytes(last_peers if final else peers.at[k], peer_send.at[k])

        @pl.when(has_after)
        def _():
            wait_bytes(last_before.at[0] if final else before.at[k], before_send.at[k])

        if not final:

            @pl.when(has_before)
            def _():
                wait_bytes(after.at[k], after_send.at[k])

    wait_bytes(sums_in.at[pl.ds(0, devices - 1)], sums_send)


def shards(blocks, blk_row, blk_col, counts, bias, mask):
    rows, subs = lax.axis_size("row"), lax.axis_size("sub")
    slots = blocks.shape[0]
    own = bias.shape[0] // LANES
    group = own * subs
    span = group + TILE
    mid = ITERS - 1
    f32, bf16 = jnp.float32, jnp.bfloat16
    dma = pltpu.SemaphoreType.DMA
    vmem = pl.BlockSpec(memory_space=pltpu.VMEM)
    def pin(x):
        return pltpu.with_memory_space_constraint(x, pltpu.HBM)

    both = pl.pallas_call(
        kernel,
        out_shape=pltpu.VMEM((2, own, LANES), f32),
        in_specs=[pl.BlockSpec(memory_space=pltpu.HBM)] * 6,
        out_specs=vmem,
        scratch_shapes=[
            pltpu.SMEM((slots,), jnp.int32),
            pltpu.SMEM((slots,), jnp.int32),
            pltpu.SMEM((1,), jnp.int32),
            pltpu.VMEM((own, LANES), f32),
            pltpu.VMEM((own, LANES), jnp.int32),
            pltpu.VMEM(blocks.shape, bf16),
            pltpu.VMEM(blocks.shape, bf16),
            pltpu.VMEM((LEAD + PAD * PIECES + TILE, LANES), f32),
            pltpu.VMEM((TILE, LANES), f32),
            pltpu.VMEM((ITERS, span, LANES), f32),
            pltpu.VMEM((mid, subs - 1, span, LANES), f32),
            pltpu.VMEM((mid, subs, TILE, LANES), f32),
            pltpu.VMEM((mid, subs, TILE, LANES), f32),
            pltpu.VMEM((subs - 1, own, LANES), f32),
            pltpu.VMEM((subs, TILE, LANES), f32),
            pltpu.VMEM((2, LANES), f32),
            pltpu.VMEM((rows * subs, 2, LANES), f32),
            pltpu.VMEM((slots, 2 * PAD, LANES), bf16),
            pltpu.VMEM((slots, 2 * PAD, LANES), bf16),
            pltpu.VMEM((slots, 2 * PAD, LANES), bf16),
            pltpu.VMEM((2 * PAD, LANES), bf16),
            dma((5,)),
            dma((slots,)),
            dma((subs - 1,)),
            dma((subs - 1,)),
            dma((subs,)),
            dma,
            dma((ITERS,)),
            dma((ITERS,)),
            dma((ITERS,)),
            dma((ITERS,)),
            dma((mid,)),
            dma((mid,)),
            dma,
            dma,
            pltpu.SemaphoreType.REGULAR((max((rows - 1).bit_length(), 1),)),
            pltpu.SemaphoreType.REGULAR,
        ],
        compiler_params=pltpu.CompilerParams(
            collective_id=0, has_side_effects=True, vmem_limit_bytes=40 * 1024 * 1024
        ),
    )(pin(blk_row), pin(blk_col), counts, pin(bias.reshape(own, LANES)), pin(mask.reshape(own, LANES)), pin(blocks))
    balanced, coverage = both[0], both[1]
    return balanced.reshape(-1), coverage.reshape(-1)


def solution(mesh):
    everywhere = P(("row", "sub"))
    return jax.shard_map(
        shards,
        mesh=mesh,
        in_specs=(P(("row", "sub"), None, None),) + (everywhere,) * 5,
        out_specs=(everywhere, everywhere),
        check_vma=False,
    )
```

```python
import functools

import jax
import jax.numpy as jnp
from jax import lax
from jax.experimental import pallas as pl
from jax.experimental.pallas import tpu as pltpu
from jax.sharding import PartitionSpec as P

BLK = 512
ITERS = 3
LANES = 128
PIECES = BLK // LANES
TILE = 8
PAD = 8
LEAD = TILE
LATE = 2
LINK = 1


def kernel(
    row_hbm, col_hbm, count_hbm, bias_hbm, mask_hbm, blocks_ref, both_ref,
    row_ref, col_ref, count_ref, bias_ref, mask_ref, held, turned, weights, follow, part, peers, before, after, last_peers, last_before, sums_out, sums_in, mask_a, mask_c, mask_r, mask_e,
    small_sem, load_sem, gather_send, gather_recv, edge_send, edge_recv, peer_send, peer_recv,
    before_send, before_recv, after_send, after_recv, sums_send, sums_recv, known, ready,
):
    rows, subs = lax.axis_size("row"), lax.axis_size("sub")
    devices = rows * subs
    row, sub = lax.axis_index("row"), lax.axis_index("sub")
    slots = held.shape[0]
    own = bias_ref.shape[0]
    group = own * subs
    span = group + TILE
    has_before, has_after = row > 0, row < rows - 1

    def remote(src, dst, send, recv, target_row, target_sub):
        return pltpu.make_async_remote_copy(
            src_ref=src, dst_ref=dst, send_sem=send, recv_sem=recv,
            device_id=(target_row, target_sub), device_id_type=pl.DeviceIdType.MESH,
        )

    def wait_bytes(ref, sem):
        pltpu.make_async_copy(ref, ref, sem).wait()

    def ring(offset):
        return lax.rem(sub + offset, subs)

    others = sorted(range(1, subs), key=lambda offset: -min(offset, subs - offset))
    loads = [pltpu.make_async_copy(blocks_ref.at[s], held.at[s], load_sem.at[s]) for s in range(slots)]
    smalls = [
        pltpu.make_async_copy(src, dst, small_sem.at[i])
        for i, (src, dst) in enumerate(
            ((bias_hbm, bias_ref), (mask_hbm, mask_ref), (row_hbm, row_ref), (col_hbm, col_ref), (count_hbm, count_ref))
        )
    ]
    barrier = pltpu.get_barrier_semaphore()

    def greet(target_row, target_sub, sem=barrier):
        pl.semaphore_signal(sem, inc=1, device_id=(target_row, target_sub), device_id_type=pl.DeviceIdType.MESH)

    for offset in others:
        greet(row, ring(offset))
    for load in smalls:
        load.start()

    @pl.when(has_after)
    def _():
        greet(row + 1, LINK)

    for load in loads:
        load.start()

    stages = (rows - 1).bit_length()

    def tell(j):
        reach = 2**j

        @pl.when(row >= reach)
        def _():
            greet(row - reach, sub, known.at[j])

        @pl.when(row + reach < rows)
        def _():
            greet(row + reach, sub, known.at[j])

    def hear(j):
        reach = 2**j
        pl.semaphore_wait(known.at[j], jnp.where(row >= reach, 1, 0) + jnp.where(row + reach < rows, 1, 0))

    weights[0:LEAD, :] = jnp.zeros((LEAD, LANES), jnp.float32)
    rest = weights.shape[0] - LEAD - group
    weights[LEAD + group :, :] = jnp.zeros((rest, LANES), jnp.float32)
    for k in range(ITERS):
        part[k, group:span, :] = jnp.zeros((TILE, LANES), jnp.float32)

    @pl.when(jnp.logical_not(has_after))
    def _():
        follow[...] = jnp.zeros_like(follow)
        after[...] = jnp.zeros_like(after)

    @pl.when(jnp.logical_not(has_before))
    def _():
        before[...] = jnp.zeros_like(before)
        last_before[...] = jnp.zeros_like(last_before)

    @pl.when(jnp.logical_and(has_before, sub > 0))
    def _():
        last_before[...] = jnp.zeros_like(last_before)

    smalls[0].wait()
    smalls[1].wait()
    own_live = mask_ref[...].astype(jnp.float32)
    mine = pl.ds(pl.multiple_of(LEAD + sub * own, TILE), own)
    weights[mine, :] = bias_ref[...] * own_live

    linked = jnp.logical_and(has_before, sub == LINK)
    pl.semaphore_wait(barrier, subs - 1 + jnp.where(linked, subs, 0))

    for offset in others:
        remote(
            weights.at[mine], weights.at[mine], gather_send.at[offset - 1], gather_recv.at[offset - 1], row, ring(offset)
        ).start()

    @pl.when(linked)
    def _():
        for target in range(subs):
            greet(row - 1, target, ready)

    for load in smalls[2:]:
        load.wait()
    first_block = row * (group // PIECES)
    next_block = first_block + group // PIECES
    ids = lax.broadcasted_iota(jnp.int32, (PAD, LANES), 0)
    leaves, enters = [], []
    for s in range(slots):
        lives = s < count_ref[0]
        leaves.append(jnp.where(jnp.logical_and(lives, col_ref[s] == next_block), 1, 0))
        enters.append(jnp.where(jnp.logical_and(lives, row_ref[s] == first_block), 1, 0))
    leavers = sum(leaves)
    leaving = leavers.astype(jnp.float32)
    seen, seen_last = leavers, slots - sum(enters)
    order = [0] * slots
    for s in range(slots):
        place = jnp.where(leaves[s] == 1, 0, jnp.where(enters[s] == 1, seen_last, seen))
        for i in range(slots):
            order[i] = order[i] + jnp.where(place == i, s, 0)
        seen = seen + 1 - leaves[s] - enters[s]
        seen_last = seen_last + enters[s]
    for s in range(slots):
        p = row_ref[order[s]] - first_block
        q = col_ref[order[s]] - first_block
        alive = jnp.where(order[s] < count_ref[0], 1.0, 0.0).astype(jnp.float32)
        same = jnp.where(p == q, 1.0, 0.0).astype(jnp.float32)
        at_p = jnp.where(ids == p, 1.0, 0.0).astype(jnp.float32)
        at_q = jnp.where(ids == q, 1.0, 0.0).astype(jnp.float32)
        for ref, value in (
            (mask_a, at_p * (0.5 * alive * same)),
            (mask_c, at_q * (alive * (1.0 - same))),
            (mask_r, at_p * (alive * (1.0 - same))),
        ):
            value = value.astype(jnp.bfloat16)
            ref[s] = jnp.concatenate([value, value], axis=0)
    value = (jnp.where(ids == group // PIECES - 1, 1.0, 0.0).astype(jnp.float32) * leaving).astype(jnp.bfloat16)
    mask_e[...] = jnp.concatenate([value, value], axis=0)

    first_own = weights.at[pl.ds(LEAD, own)]

    @pl.when(linked)
    def _():
        wait_bytes(first_own, gather_recv.at[LINK - 1])
        for target in range(subs):
            remote(
                weights.at[pl.ds(LEAD, TILE)], follow,
                edge_send.at[target], edge_recv, row - 1, target,
            ).start()

    @pl.loop(0, slots)
    def _(s):
        pltpu.make_async_copy(blocks_ref.at[s], held.at[s], load_sem.at[s]).wait()
        turned[s] = held[s].T

    for offset in range(1, subs):
        theirs = weights.at[pl.ds(pl.multiple_of(LEAD + ring(subs - offset) * own, TILE), own)]
        if offset == LINK:

            @pl.when(jnp.logical_not(linked))
            def _():
                wait_bytes(theirs, gather_recv.at[offset - 1])
        else:
            wait_bytes(theirs, gather_recv.at[offset - 1])

    top = lax.broadcasted_iota(jnp.int32, (TILE, LANES), 0) < PIECES
    inner = weights[LEAD : LEAD + group, :]
    alive = inner > 0.0
    totals = []
    lane = lax.broadcasted_iota(jnp.int32, (1, LANES), 1)
    kept = jnp.sum(jnp.sum(own_live, axis=0, keepdims=True), axis=1, keepdims=True)

    def blocked(start):
        return jnp.concatenate(
            [weights[pl.ds(LEAD + start + q, PAD, stride=PIECES), :] for q in range(PIECES)], axis=1
        )

    def operand(start):
        value = blocked(start)
        high = value.astype(jnp.bfloat16)
        low = (value - high.astype(jnp.float32)).astype(jnp.bfloat16)
        return jnp.concatenate([high, low], axis=0)

    def wide(mask):
        return jnp.concatenate([mask] * PIECES, axis=1)

    def dot(left, right):
        return lax.dot_general(left, right, (((1,), (0,)), ((), ())), preferred_element_type=jnp.float32)

    edge_rows = pl.ds(group, TILE)
    last_slots = min(LATE, slots - 1)

    for k in range(ITERS):
        final = k == ITERS - 1
        here, lower, upper = operand(0), operand(-PIECES), operand(PIECES)
        first = dot(wide(mask_a[0] + mask_e[...]) * here + wide(mask_c[0]) * lower, held[order[0]])
        total = first * (1.0 - leaving)
        for s in range(1, slots):
            if s == slots - last_slots:
                if k == 0:

                    @pl.when(has_after)
                    def _():
                        wait_bytes(follow, edge_recv)

                    back = jnp.where(top, follow[...], 0.0)
                    back_live = back > 0.0
                else:

                    @pl.when(has_after)
                    def _():
                        wait_bytes(after.at[k - 1], after_recv.at[k - 1])

                    @pl.when(has_before)
                    def _():
                        wait_bytes(before.at[k - 1], before_recv.at[k - 1])

                    back = jnp.where(back_live, 1.0 / (back_sums + jnp.sum(after[k - 1], axis=0)), 0.0)
                    front = front_sums + jnp.where(top, jnp.sum(before[k - 1], axis=0), 0.0)
                    front = jnp.where(alive[:TILE], 1.0 / front, 0.0)
                    inner = jnp.concatenate([front, inner[TILE:]], axis=0)
                    weights[LEAD : LEAD + TILE, :] = front
                weights[LEAD + group : LEAD + span, :] = back
                whole = jnp.concatenate([inner, back], axis=0)
                here, lower, upper = operand(0), operand(-PIECES), operand(PIECES)
            on = wide(mask_a[s]) * here
            total += dot(on + wide(mask_c[s]) * lower, held[order[s]])
            total += dot(on + wide(mask_r[s]) * upper, turned[order[s]])
            if s == 1:
                out = (first[PAD - 1 : PAD] + first[2 * PAD - 1 : 2 * PAD]) * leaving
                for q in range(PIECES):
                    part[k, group + q : group + q + 1, :] = out[:, q * LANES : (q + 1) * LANES]

                if k == 0:

                    @pl.when(has_after)
                    def _():
                        pl.semaphore_wait(ready, 1)

                    if stages:
                        tell(0)

                @pl.when(has_after)
                def _():
                    if final:
                        remote(
                            part.at[k, edge_rows], last_before.at[sub], before_send.at[k], before_recv.at[k], row + 1, 0
                        ).start()
                    else:
                        for offset in range(subs):
                            remote(
                                part.at[k, edge_rows], before.at[k, offset], before_send.at[k], before_recv.at[k],
                                row + 1, ring(offset),
                            ).start()

        total += dot(wide(mask_a[0]) * here + wide(mask_r[0]) * upper, turned[order[0]])
        total = total[:PAD] + total[PAD:]

        def keep():
            for q in range(PIECES):
                part[k, pl.ds(q, PAD, stride=PIECES), :] = total[:, q * LANES : (q + 1) * LANES]

        if not final:
            keep()
            for offset in others:
                remote(
                    part.at[k, pl.ds(0, span)], peers.at[k, offset - 1],
                    peer_send.at[k], peer_recv.at[k], row, ring(offset),
                ).start()

            @pl.when(has_before)
            def _():
                for offset in range(subs):
                    remote(
                        part.at[k, pl.ds(0, TILE)], after.at[k, offset], after_send.at[k], after_recv.at[k],
                        row - 1, ring(offset),
                    ).start()

            if k < stages:
                hear(k)
            if k + 1 < stages:
                tell(k + 1)
            product = whole * part[k, 0:span, :]
            totals.append(jnp.sum(jnp.sum(product, axis=0, keepdims=True), axis=1, keepdims=True))
            if k == 0:
                for offset in range(1, subs):
                    wait_bytes(weights.at[mine], gather_send.at[offset - 1])

                @pl.when(linked)
                def _():
                    for target in range(subs):
                        wait_bytes(weights.at[pl.ds(LEAD, TILE)], edge_send.at[target])

            wait_bytes(peers.at[k], peer_recv.at[k])
            sums = part[k, 0:span, :]
            for offset in range(1, subs):
                sums += peers[k, offset - 1]
            front_sums, back_sums = sums[:TILE], sums[group:]
            inner = jnp.where(alive, 1.0 / sums[:group], 0.0)
            weights[LEAD : LEAD + group, :] = inner
        else:
            scalars = jnp.zeros((1, LANES), jnp.float32)
            for i, value in enumerate(totals + [kept]):
                scalars = jnp.where(lane == i, value, scalars)
            sums_out[1:2, :] = scalars
            for j in range(k, stages):
                hear(j)
                if j + 1 < stages:
                    tell(j + 1)
            product = back * part[k, group:span, :]
            blocked_product = blocked(0) * total
            for q in range(PIECES):
                product += blocked_product[:, q * LANES : (q + 1) * LANES]
            sums_out[0:1, :] = jnp.sum(product, axis=0, keepdims=True)

            keep()
            for offset in others:
                theirs = pl.ds(pl.multiple_of(ring(offset) * own, TILE), own)
                remote(
                    part.at[k, theirs], last_peers.at[offset - 1], peer_send.at[k], peer_recv.at[k], row, ring(offset)
                ).start()

            @pl.loop(0, rows)
            def _(target_row):
                for offset in others:
                    remote(
                        sums_out, sums_in.at[row * subs + offset], sums_send, sums_recv, target_row, ring(offset)
                    ).start()

                @pl.when(target_row != row)
                def _():
                    remote(sums_out, sums_in.at[row * subs], sums_send, sums_recv, target_row, sub).start()

            wait_bytes(last_peers, peer_recv.at[k])

            @pl.when(jnp.logical_and(has_before, sub == 0))
            def _():
                wait_bytes(last_before, before_recv.at[k])

            sums = part[k, pl.ds(pl.multiple_of(sub * own, TILE), own), :] + jnp.sum(last_peers[...], axis=0)
            front = jnp.where(top, jnp.sum(last_before[...], axis=0), 0.0)
            if own > TILE:
                front = jnp.concatenate([front, jnp.zeros((own - TILE, LANES), jnp.float32)], axis=0)
            sums = sums + front
            now = weights[mine, :]
            inverse = jnp.where(own_live > 0.0, 1.0 / sums, 0.0)
            scaled = now * sums
            everyone = sums_in.at[pl.ds(0, devices - 1)]
            wait_bytes(everyone, sums_recv)
            sums_in[row * subs] = sums_out[...]
            grand = jnp.sum(sums_in[...], axis=0)
            bins = grand[1:2, ITERS - 1 : ITERS]
            all_scaled = jnp.sum(grand[0:1], axis=1, keepdims=True)
            scale = all_scaled / bins
            for i in range(ITERS - 1):
                scale = scale * (grand[1:2, i : i + 1] / bins)
            both_ref[1] = scaled * (bins / all_scaled)
            both_ref[0] = scale * inverse

    for k in range(ITERS):
        final = k == ITERS - 1
        wait_bytes(last_peers if final else peers.at[k], peer_send.at[k])

        @pl.when(has_after)
        def _():
            wait_bytes(last_before.at[0] if final else before.at[k], before_send.at[k])

        if not final:

            @pl.when(has_before)
            def _():
                wait_bytes(after.at[k], after_send.at[k])

    wait_bytes(sums_in.at[pl.ds(0, devices - 1)], sums_send)


def shards(blocks, blk_row, blk_col, counts, bias, mask):
    rows, subs = lax.axis_size("row"), lax.axis_size("sub")
    slots = blocks.shape[0]
    own = bias.shape[0] // LANES
    group = own * subs
    span = group + TILE
    mid = ITERS - 1
    f32, bf16 = jnp.float32, jnp.bfloat16
    dma = pltpu.SemaphoreType.DMA
    vmem = pl.BlockSpec(memory_space=pltpu.VMEM)
    def pin(x):
        return pltpu.with_memory_space_constraint(x, pltpu.HBM)

    both = pl.pallas_call(
        kernel,
        out_shape=pltpu.VMEM((2, own, LANES), f32),
        in_specs=[pl.BlockSpec(memory_space=pltpu.HBM)] * 6,
        out_specs=vmem,
        scratch_shapes=[
            pltpu.SMEM((slots,), jnp.int32),
            pltpu.SMEM((slots,), jnp.int32),
            pltpu.SMEM((1,), jnp.int32),
            pltpu.VMEM((own, LANES), f32),
            pltpu.VMEM((own, LANES), jnp.int32),
            pltpu.VMEM(blocks.shape, bf16),
            pltpu.VMEM(blocks.shape, bf16),
            pltpu.VMEM((LEAD + PAD * PIECES + TILE, LANES), f32),
            pltpu.VMEM((TILE, LANES), f32),
            pltpu.VMEM((ITERS, span, LANES), f32),
            pltpu.VMEM((mid, subs - 1, span, LANES), f32),
            pltpu.VMEM((mid, subs, TILE, LANES), f32),
            pltpu.VMEM((mid, subs, TILE, LANES), f32),
            pltpu.VMEM((subs - 1, own, LANES), f32),
            pltpu.VMEM((subs, TILE, LANES), f32),
            pltpu.VMEM((2, LANES), f32),
            pltpu.VMEM((rows * subs, 2, LANES), f32),
            pltpu.VMEM((slots, 2 * PAD, LANES), bf16),
            pltpu.VMEM((slots, 2 * PAD, LANES), bf16),
            pltpu.VMEM((slots, 2 * PAD, LANES), bf16),
            pltpu.VMEM((2 * PAD, LANES), bf16),
            dma((5,)),
            dma((slots,)),
            dma((subs - 1,)),
            dma((subs - 1,)),
            dma((subs,)),
            dma,
            dma((ITERS,)),
            dma((ITERS,)),
            dma((ITERS,)),
            dma((ITERS,)),
            dma((mid,)),
            dma((mid,)),
            dma,
            dma,
            pltpu.SemaphoreType.REGULAR((max((rows - 1).bit_length(), 1),)),
            pltpu.SemaphoreType.REGULAR,
        ],
        compiler_params=pltpu.CompilerParams(
            collective_id=0, has_side_effects=True, vmem_limit_bytes=40 * 1024 * 1024
        ),
    )(pin(blk_row), pin(blk_col), counts, pin(bias.reshape(own, LANES)), pin(mask.reshape(own, LANES)), pin(blocks))
    balanced, coverage = both[0], both[1]
    return balanced.reshape(-1), coverage.reshape(-1)


def solution(mesh):
    everywhere = P(("row", "sub"))
    return jax.shard_map(
        shards,
        mesh=mesh,
        in_specs=(P(("row", "sub"), None, None),) + (everywhere,) * 5,
        out_specs=(everywhere, everywhere),
        check_vma=False,
    )
```

```python
import functools

import jax
import jax.numpy as jnp
from jax import lax
from jax.experimental import pallas as pl
from jax.experimental.pallas import tpu as pltpu
from jax.sharding import PartitionSpec as P

BLK = 512
ITERS = 3
LANES = 128
PIECES = BLK // LANES
TILE = 8
PAD = 8
LEAD = TILE
LATE = 2
LINK = 1


def kernel(
    row_hbm, col_hbm, count_hbm, bias_hbm, mask_hbm, blocks_ref, both_ref,
    row_ref, col_ref, count_ref, bias_ref, mask_ref, held, turned, weights, follow, part, peers, before, after, last_peers, last_before, sums_out, sums_in, mask_a, mask_c, mask_r, mask_e,
    small_sem, load_sem, gather_send, gather_recv, edge_send, edge_recv, peer_send, peer_recv,
    before_send, before_recv, after_send, after_recv, sums_send, sums_recv, known, ready,
):
    rows, subs = lax.axis_size("row"), lax.axis_size("sub")
    devices = rows * subs
    row, sub = lax.axis_index("row"), lax.axis_index("sub")
    slots = held.shape[0]
    own = bias_ref.shape[0]
    group = own * subs
    span = group + TILE
    has_before, has_after = row > 0, row < rows - 1

    def remote(src, dst, send, recv, target_row, target_sub):
        return pltpu.make_async_remote_copy(
            src_ref=src, dst_ref=dst, send_sem=send, recv_sem=recv,
            device_id=(target_row, target_sub), device_id_type=pl.DeviceIdType.MESH,
        )

    def wait_bytes(ref, sem):
        pltpu.make_async_copy(ref, ref, sem).wait()

    def ring(offset):
        return lax.rem(sub + offset, subs)

    others = sorted(range(1, subs), key=lambda offset: -min(offset, subs - offset))
    loads = [pltpu.make_async_copy(blocks_ref.at[s], held.at[s], load_sem.at[s]) for s in range(slots)]
    smalls = [
        pltpu.make_async_copy(src, dst, small_sem.at[i])
        for i, (src, dst) in enumerate(
            ((bias_hbm, bias_ref), (mask_hbm, mask_ref), (row_hbm, row_ref), (col_hbm, col_ref), (count_hbm, count_ref))
        )
    ]
    barrier = pltpu.get_barrier_semaphore()

    def greet(target_row, target_sub, sem=barrier):
        pl.semaphore_signal(sem, inc=1, device_id=(target_row, target_sub), device_id_type=pl.DeviceIdType.MESH)

    for offset in others:
        greet(row, ring(offset))
    for load in smalls:
        load.start()

    @pl.when(has_after)
    def _():
        greet(row + 1, LINK)

    for load in loads:
        load.start()

    stages = (rows - 1).bit_length()

    def tell(j):
        reach = 2**j

        @pl.when(row >= reach)
        def _():
            greet(row - reach, sub, known.at[j])

        @pl.when(row + reach < rows)
        def _():
            greet(row + reach, sub, known.at[j])

    def hear(j):
        reach = 2**j
        pl.semaphore_wait(known.at[j], jnp.where(row >= reach, 1, 0) + jnp.where(row + reach < rows, 1, 0))

    weights[0:LEAD, :] = jnp.zeros((LEAD, LANES), jnp.float32)
    rest = weights.shape[0] - LEAD - group
    weights[LEAD + group :, :] = jnp.zeros((rest, LANES), jnp.float32)
    for k in range(ITERS):
        part[k, group:span, :] = jnp.zeros((TILE, LANES), jnp.float32)

    @pl.when(jnp.logical_not(has_after))
    def _():
        follow[...] = jnp.zeros_like(follow)
        after[...] = jnp.zeros_like(after)

    @pl.when(jnp.logical_not(has_before))
    def _():
        before[...] = jnp.zeros_like(before)
        last_before[...] = jnp.zeros_like(last_before)

    @pl.when(jnp.logical_and(has_before, sub > 0))
    def _():
        last_before[...] = jnp.zeros_like(last_before)

    smalls[0].wait()
    smalls[1].wait()
    own_live = mask_ref[...].astype(jnp.float32)
    mine = pl.ds(pl.multiple_of(LEAD + sub * own, TILE), own)
    weights[mine, :] = bias_ref[...] * own_live

    linked = jnp.logical_and(has_before, sub == LINK)
    pl.semaphore_wait(barrier, subs - 1 + jnp.where(linked, subs, 0))

    for offset in others:
        remote(
            weights.at[mine], weights.at[mine], gather_send.at[offset - 1], gather_recv.at[offset - 1], row, ring(offset)
        ).start()

    @pl.when(linked)
    def _():
        for target in range(subs):
            greet(row - 1, target, ready)

    for load in smalls[2:]:
        load.wait()
    first_block = row * (group // PIECES)
    next_block = first_block + group // PIECES
    ids = lax.broadcasted_iota(jnp.int32, (PAD, LANES), 0)
    leaves, enters = [], []
    for s in range(slots):
        lives = s < count_ref[0]
        leaves.append(jnp.where(jnp.logical_and(lives, col_ref[s] == next_block), 1, 0))
        enters.append(jnp.where(jnp.logical_and(lives, row_ref[s] == first_block), 1, 0))
    leavers = sum(leaves)
    leaving = leavers.astype(jnp.float32)
    seen, seen_last = leavers, slots - sum(enters)
    order = [0] * slots
    for s in range(slots):
        place = jnp.where(leaves[s] == 1, 0, jnp.where(enters[s] == 1, seen_last, seen))
        for i in range(slots):
            order[i] = order[i] + jnp.where(place == i, s, 0)
        seen = seen + 1 - leaves[s] - enters[s]
        seen_last = seen_last + enters[s]
    for s in range(slots):
        p = row_ref[order[s]] - first_block
        q = col_ref[order[s]] - first_block
        alive = jnp.where(order[s] < count_ref[0], 1.0, 0.0).astype(jnp.float32)
        same = jnp.where(p == q, 1.0, 0.0).astype(jnp.float32)
        at_p = jnp.where(ids == p, 1.0, 0.0).astype(jnp.float32)
        at_q = jnp.where(ids == q, 1.0, 0.0).astype(jnp.float32)
        for ref, value in (
            (mask_a, at_p * (0.5 * alive * same)),
            (mask_c, at_q * (alive * (1.0 - same))),
            (mask_r, at_p * (alive * (1.0 - same))),
        ):
            value = value.astype(jnp.bfloat16)
            ref[s] = jnp.concatenate([value, value], axis=0)
    value = (jnp.where(ids == group // PIECES - 1, 1.0, 0.0).astype(jnp.float32) * leaving).astype(jnp.bfloat16)
    mask_e[...] = jnp.concatenate([value, value], axis=0)

    first_own = weights.at[pl.ds(LEAD, own)]

    @pl.when(linked)
    def _():
        wait_bytes(first_own, gather_recv.at[LINK - 1])
        for target in range(subs):
            remote(
                weights.at[pl.ds(LEAD, TILE)], follow,
                edge_send.at[target], edge_recv, row - 1, target,
            ).start()

    @pl.loop(0, slots)
    def _(s):
        pltpu.make_async_copy(blocks_ref.at[s], held.at[s], load_sem.at[s]).wait()
        turned[s] = held[s].T

    for offset in range(1, subs):
        theirs = weights.at[pl.ds(pl.multiple_of(LEAD + ring(subs - offset) * own, TILE), own)]
        if offset == LINK:

            @pl.when(jnp.logical_not(linked))
            def _():
                wait_bytes(theirs, gather_recv.at[offset - 1])
        else:
            wait_bytes(theirs, gather_recv.at[offset - 1])

    top = lax.broadcasted_iota(jnp.int32, (TILE, LANES), 0) < PIECES
    inner = weights[LEAD : LEAD + group, :]
    alive = inner > 0.0
    totals = []
    lane = lax.broadcasted_iota(jnp.int32, (1, LANES), 1)
    kept = jnp.sum(jnp.sum(own_live, axis=0, keepdims=True), axis=1, keepdims=True)

    def blocked(start):
        return jnp.concatenate(
            [weights[pl.ds(LEAD + start + q, PAD, stride=PIECES), :] for q in range(PIECES)], axis=1
        )

    def operand(start):
        value = blocked(start)
        high = value.astype(jnp.bfloat16)
        low = (value - high.astype(jnp.float32)).astype(jnp.bfloat16)
        return jnp.concatenate([high, low], axis=0)

    def wide(mask):
        return jnp.concatenate([mask] * PIECES, axis=1)

    def dot(left, right):
        return lax.dot_general(left, right, (((1,), (0,)), ((), ())), preferred_element_type=jnp.float32)

    edge_rows = pl.ds(group, TILE)
    last_slots = min(LATE, slots - 1)

    for k in range(ITERS):
        final = k == ITERS - 1
        here, lower, upper = operand(0), operand(-PIECES), operand(PIECES)
        first = dot(wide(mask_a[0] + mask_e[...]) * here + wide(mask_c[0]) * lower, held[order[0]])
        total = first * (1.0 - leaving)
        for s in range(1, slots):
            if s == slots - last_slots:
                if k == 0:

                    @pl.when(has_after)
                    def _():
                        wait_bytes(follow, edge_recv)

                    back = jnp.where(top, follow[...], 0.0)
                    back_live = back > 0.0
                else:

                    @pl.when(has_after)
                    def _():
                        wait_bytes(after.at[k - 1], after_recv.at[k - 1])

                    @pl.when(has_before)
                    def _():
                        wait_bytes(before.at[k - 1], before_recv.at[k - 1])

                    back = jnp.where(back_live, 1.0 / (back_sums + jnp.sum(after[k - 1], axis=0)), 0.0)
                    front = front_sums + jnp.where(top, jnp.sum(before[k - 1], axis=0), 0.0)
                    front = jnp.where(alive[:TILE], 1.0 / front, 0.0)
                    inner = jnp.concatenate([front, inner[TILE:]], axis=0)
                    weights[LEAD : LEAD + TILE, :] = front
                weights[LEAD + group : LEAD + span, :] = back
                whole = jnp.concatenate([inner, back], axis=0)
                here, lower, upper = operand(0), operand(-PIECES), operand(PIECES)
            on = wide(mask_a[s]) * here
            total += dot(on + wide(mask_c[s]) * lower, held[order[s]])
            total += dot(on + wide(mask_r[s]) * upper, turned[order[s]])
            if s == 1:
                out = (first[PAD - 1 : PAD] + first[2 * PAD - 1 : 2 * PAD]) * leaving
                for q in range(PIECES):
                    part[k, group + q : group + q + 1, :] = out[:, q * LANES : (q + 1) * LANES]

                if k == 0:

                    @pl.when(has_after)
                    def _():
                        pl.semaphore_wait(ready, 1)

                    if stages:
                        tell(0)

                if not final:
                    for offset in others:
                        remote(
                            part.at[k, edge_rows], peers.at[k, offset - 1, edge_rows],
                            peer_send.at[k], peer_recv.at[k], row, ring(offset),
                        ).start()

                @pl.when(has_after)
                def _():
                    if final:
                        remote(
                            part.at[k, edge_rows], last_before.at[sub], before_send.at[k], before_recv.at[k], row + 1, 0
                        ).start()
                    else:
                        for offset in range(subs):
                            remote(
                                part.at[k, edge_rows], before.at[k, offset], before_send.at[k], before_recv.at[k],
                                row + 1, ring(offset),
                            ).start()

        total += dot(wide(mask_a[0]) * here + wide(mask_r[0]) * upper, turned[order[0]])
        total = total[:PAD] + total[PAD:]

        def keep():
            for q in range(PIECES):
                part[k, pl.ds(q, PAD, stride=PIECES), :] = total[:, q * LANES : (q + 1) * LANES]

        if not final:
            keep()
            for offset in others:
                remote(
                    part.at[k, pl.ds(0, group)], peers.at[k, offset - 1, pl.ds(0, group)],
                    peer_send.at[k], peer_recv.at[k], row, ring(offset),
                ).start()

            @pl.when(has_before)
            def _():
                for offset in range(subs):
                    remote(
                        part.at[k, pl.ds(0, TILE)], after.at[k, offset], after_send.at[k], after_recv.at[k],
                        row - 1, ring(offset),
                    ).start()

            if k < stages:
                hear(k)
            if k + 1 < stages:
                tell(k + 1)
            product = whole * part[k, 0:span, :]
            totals.append(jnp.sum(jnp.sum(product, axis=0, keepdims=True), axis=1, keepdims=True))
            if k == 0:
                for offset in range(1, subs):
                    wait_bytes(weights.at[mine], gather_send.at[offset - 1])

                @pl.when(linked)
                def _():
                    for target in range(subs):
                        wait_bytes(weights.at[pl.ds(LEAD, TILE)], edge_send.at[target])

            wait_bytes(peers.at[k], peer_recv.at[k])
            sums = part[k, 0:span, :]
            for offset in range(1, subs):
                sums += peers[k, offset - 1]
            front_sums, back_sums = sums[:TILE], sums[group:]
            inner = jnp.where(alive, 1.0 / sums[:group], 0.0)
            weights[LEAD : LEAD + group, :] = inner
        else:
            scalars = jnp.zeros((1, LANES), jnp.float32)
            for i, value in enumerate(totals + [kept]):
                scalars = jnp.where(lane == i, value, scalars)
            sums_out[1:2, :] = scalars
            for j in range(k, stages):
                hear(j)
                if j + 1 < stages:
                    tell(j + 1)
            product = back * part[k, group:span, :]
            blocked_product = blocked(0) * total
            for q in range(PIECES):
                product += blocked_product[:, q * LANES : (q + 1) * LANES]
            sums_out[0:1, :] = jnp.sum(product, axis=0, keepdims=True)

            keep()
            for offset in others:
                theirs = pl.ds(pl.multiple_of(ring(offset) * own, TILE), own)
                remote(
                    part.at[k, theirs], last_peers.at[offset - 1], peer_send.at[k], peer_recv.at[k], row, ring(offset)
                ).start()

            @pl.loop(0, rows)
            def _(target_row):
                for offset in others:
                    remote(
                        sums_out, sums_in.at[row * subs + offset], sums_send, sums_recv, target_row, ring(offset)
                    ).start()

                @pl.when(target_row != row)
                def _():
                    remote(sums_out, sums_in.at[row * subs], sums_send, sums_recv, target_row, sub).start()

            wait_bytes(last_peers, peer_recv.at[k])

            @pl.when(jnp.logical_and(has_before, sub == 0))
            def _():
                wait_bytes(last_before, before_recv.at[k])

            sums = part[k, pl.ds(pl.multiple_of(sub * own, TILE), own), :] + jnp.sum(last_peers[...], axis=0)
            front = jnp.where(top, jnp.sum(last_before[...], axis=0), 0.0)
            if own > TILE:
                front = jnp.concatenate([front, jnp.zeros((own - TILE, LANES), jnp.float32)], axis=0)
            sums = sums + front
            now = weights[mine, :]
            inverse = jnp.where(own_live > 0.0, 1.0 / sums, 0.0)
            scaled = now * sums
            everyone = sums_in.at[pl.ds(0, devices - 1)]
            wait_bytes(everyone, sums_recv)
            sums_in[row * subs] = sums_out[...]
            grand = jnp.sum(sums_in[...], axis=0)
            bins = grand[1:2, ITERS - 1 : ITERS]
            all_scaled = jnp.sum(grand[0:1], axis=1, keepdims=True)
            scale = all_scaled / bins
            for i in range(ITERS - 1):
                scale = scale * (grand[1:2, i : i + 1] / bins)
            both_ref[1] = scaled * (bins / all_scaled)
            both_ref[0] = scale * inverse

    for k in range(ITERS):
        final = k == ITERS - 1
        wait_bytes(last_peers if final else peers.at[k], peer_send.at[k])

        @pl.when(has_after)
        def _():
            wait_bytes(last_before.at[0] if final else before.at[k], before_send.at[k])

        if not final:

            @pl.when(has_before)
            def _():
                wait_bytes(after.at[k], after_send.at[k])

    wait_bytes(sums_in.at[pl.ds(0, devices - 1)], sums_send)


def shards(blocks, blk_row, blk_col, counts, bias, mask):
    rows, subs = lax.axis_size("row"), lax.axis_size("sub")
    slots = blocks.shape[0]
    own = bias.shape[0] // LANES
    group = own * subs
    span = group + TILE
    mid = ITERS - 1
    f32, bf16 = jnp.float32, jnp.bfloat16
    dma = pltpu.SemaphoreType.DMA
    vmem = pl.BlockSpec(memory_space=pltpu.VMEM)
    def pin(x):
        return pltpu.with_memory_space_constraint(x, pltpu.HBM)

    both = pl.pallas_call(
        kernel,
        out_shape=pltpu.VMEM((2, own, LANES), f32),
        in_specs=[pl.BlockSpec(memory_space=pltpu.HBM)] * 6,
        out_specs=vmem,
        scratch_shapes=[
            pltpu.SMEM((slots,), jnp.int32),
            pltpu.SMEM((slots,), jnp.int32),
            pltpu.SMEM((1,), jnp.int32),
            pltpu.VMEM((own, LANES), f32),
            pltpu.VMEM((own, LANES), jnp.int32),
            pltpu.VMEM(blocks.shape, bf16),
            pltpu.VMEM(blocks.shape, bf16),
            pltpu.VMEM((LEAD + PAD * PIECES + TILE, LANES), f32),
            pltpu.VMEM((TILE, LANES), f32),
            pltpu.VMEM((ITERS, span, LANES), f32),
            pltpu.VMEM((mid, subs - 1, span, LANES), f32),
            pltpu.VMEM((mid, subs, TILE, LANES), f32),
            pltpu.VMEM((mid, subs, TILE, LANES), f32),
            pltpu.VMEM((subs - 1, own, LANES), f32),
            pltpu.VMEM((subs, TILE, LANES), f32),
            pltpu.VMEM((2, LANES), f32),
            pltpu.VMEM((rows * subs, 2, LANES), f32),
            pltpu.VMEM((slots, 2 * PAD, LANES), bf16),
            pltpu.VMEM((slots, 2 * PAD, LANES), bf16),
            pltpu.VMEM((slots, 2 * PAD, LANES), bf16),
            pltpu.VMEM((2 * PAD, LANES), bf16),
            dma((5,)),
            dma((slots,)),
            dma((subs - 1,)),
            dma((subs - 1,)),
            dma((subs,)),
            dma,
            dma((ITERS,)),
            dma((ITERS,)),
            dma((ITERS,)),
            dma((ITERS,)),
            dma((mid,)),
            dma((mid,)),
            dma,
            dma,
            pltpu.SemaphoreType.REGULAR((max((rows - 1).bit_length(), 1),)),
            pltpu.SemaphoreType.REGULAR,
        ],
        compiler_params=pltpu.CompilerParams(
            collective_id=0, has_side_effects=True, vmem_limit_bytes=40 * 1024 * 1024
        ),
    )(pin(blk_row), pin(blk_col), counts, pin(bias.reshape(own, LANES)), pin(mask.reshape(own, LANES)), pin(blocks))
    balanced, coverage = both[0], both[1]
    return balanced.reshape(-1), coverage.reshape(-1)


def solution(mesh):
    everywhere = P(("row", "sub"))
    return jax.shard_map(
        shards,
        mesh=mesh,
        in_specs=(P(("row", "sub"), None, None),) + (everywhere,) * 5,
        out_specs=(everywhere, everywhere),
        check_vma=False,
    )
```

```python
import functools

import jax
import jax.numpy as jnp
from jax import lax
from jax.experimental import pallas as pl
from jax.experimental.pallas import tpu as pltpu
from jax.sharding import PartitionSpec as P

BLK = 512
ITERS = 3
LANES = 128
PIECES = BLK // LANES
TILE = 8
PAD = 8
LEAD = TILE
LATE = 2
LINK = 1


def kernel(
    row_hbm, col_hbm, count_hbm, bias_hbm, mask_hbm, blocks_ref, both_ref,
    row_ref, col_ref, count_ref, bias_ref, mask_ref, held, turned, weights, follow, part, peers, before, after, last_peers, last_before, sums_out, sums_in, mask_a, mask_c, mask_r, mask_e,
    small_sem, load_sem, gather_send, gather_recv, edge_send, edge_recv, peer_send, peer_recv,
    before_send, before_recv, after_send, after_recv, sums_send, sums_recv, known, ready,
):
    rows, subs = lax.axis_size("row"), lax.axis_size("sub")
    devices = rows * subs
    row, sub = lax.axis_index("row"), lax.axis_index("sub")
    slots = held.shape[0]
    own = bias_ref.shape[0]
    group = own * subs
    span = group + TILE
    has_before, has_after = row > 0, row < rows - 1

    def remote(src, dst, send, recv, target_row, target_sub):
        return pltpu.make_async_remote_copy(
            src_ref=src, dst_ref=dst, send_sem=send, recv_sem=recv,
            device_id=(target_row, target_sub), device_id_type=pl.DeviceIdType.MESH,
        )

    def wait_bytes(ref, sem):
        pltpu.make_async_copy(ref, ref, sem).wait()

    def ring(offset):
        return lax.rem(sub + offset, subs)

    others = sorted(range(1, subs), key=lambda offset: -min(offset, subs - offset))
    loads = [pltpu.make_async_copy(blocks_ref.at[s], held.at[s], load_sem.at[s]) for s in range(slots)]
    smalls = [
        pltpu.make_async_copy(src, dst, small_sem.at[i])
        for i, (src, dst) in enumerate(
            ((bias_hbm, bias_ref), (mask_hbm, mask_ref), (row_hbm, row_ref), (col_hbm, col_ref), (count_hbm, count_ref))
        )
    ]
    barrier = pltpu.get_barrier_semaphore()

    def greet(target_row, target_sub, sem=barrier):
        pl.semaphore_signal(sem, inc=1, device_id=(target_row, target_sub), device_id_type=pl.DeviceIdType.MESH)

    for offset in others:
        greet(row, ring(offset))
    for load in smalls:
        load.start()

    @pl.when(has_after)
    def _():
        greet(row + 1, LINK)

    for load in loads:
        load.start()

    stages = (rows - 1).bit_length()

    def tell(j):
        reach = 2**j

        @pl.when(row >= reach)
        def _():
            greet(row - reach, sub, known.at[j])

        @pl.when(row + reach < rows)
        def _():
            greet(row + reach, sub, known.at[j])

    def hear(j):
        reach = 2**j
        pl.semaphore_wait(known.at[j], jnp.where(row >= reach, 1, 0) + jnp.where(row + reach < rows, 1, 0))

    weights[0:LEAD, :] = jnp.zeros((LEAD, LANES), jnp.float32)
    rest = weights.shape[0] - LEAD - group
    weights[LEAD + group :, :] = jnp.zeros((rest, LANES), jnp.float32)
    for k in range(ITERS):
        part[k, group:span, :] = jnp.zeros((TILE, LANES), jnp.float32)

    @pl.when(jnp.logical_not(has_after))
    def _():
        follow[...] = jnp.zeros_like(follow)
        after[...] = jnp.zeros_like(after)

    @pl.when(jnp.logical_not(has_before))
    def _():
        before[...] = jnp.zeros_like(before)
        last_before[...] = jnp.zeros_like(last_before)

    @pl.when(jnp.logical_and(has_before, sub > 0))
    def _():
        last_before[...] = jnp.zeros_like(last_before)

    smalls[0].wait()
    smalls[1].wait()
    own_live = mask_ref[...].astype(jnp.float32)
    mine = pl.ds(pl.multiple_of(LEAD + sub * own, TILE), own)
    weights[mine, :] = bias_ref[...] * own_live

    linked = jnp.logical_and(has_before, sub == LINK)
    pl.semaphore_wait(barrier, subs - 1 + jnp.where(linked, subs, 0))

    for offset in others:
        remote(
            weights.at[mine], weights.at[mine], gather_send.at[offset - 1], gather_recv.at[offset - 1], row, ring(offset)
        ).start()

    @pl.when(linked)
    def _():
        for target in range(subs):
            greet(row - 1, target, ready)

    for load in smalls[2:]:
        load.wait()
    first_block = row * (group // PIECES)
    next_block = first_block + group // PIECES
    ids = lax.broadcasted_iota(jnp.int32, (PAD, LANES), 0)
    leaves, enters = [], []
    for s in range(slots):
        lives = s < count_ref[0]
        leaves.append(jnp.where(jnp.logical_and(lives, col_ref[s] == next_block), 1, 0))
        enters.append(jnp.where(jnp.logical_and(lives, row_ref[s] == first_block), 1, 0))
    leavers = sum(leaves)
    leaving = leavers.astype(jnp.float32)
    seen, seen_last = leavers, slots - sum(enters)
    order = [0] * slots
    for s in range(slots):
        place = jnp.where(leaves[s] == 1, 0, jnp.where(enters[s] == 1, seen_last, seen))
        for i in range(slots):
            order[i] = order[i] + jnp.where(place == i, s, 0)
        seen = seen + 1 - leaves[s] - enters[s]
        seen_last = seen_last + enters[s]
    for s in range(slots):
        p = row_ref[order[s]] - first_block
        q = col_ref[order[s]] - first_block
        alive = jnp.where(order[s] < count_ref[0], 1.0, 0.0).astype(jnp.float32)
        same = jnp.where(p == q, 1.0, 0.0).astype(jnp.float32)
        at_p = jnp.where(ids == p, 1.0, 0.0).astype(jnp.float32)
        at_q = jnp.where(ids == q, 1.0, 0.0).astype(jnp.float32)
        for ref, value in (
            (mask_a, at_p * (0.5 * alive * same)),
            (mask_c, at_q * (alive * (1.0 - same))),
            (mask_r, at_p * (alive * (1.0 - same))),
        ):
            value = value.astype(jnp.bfloat16)
            ref[s] = jnp.concatenate([value, value], axis=0)
    value = (jnp.where(ids == group // PIECES - 1, 1.0, 0.0).astype(jnp.float32) * leaving).astype(jnp.bfloat16)
    mask_e[...] = jnp.concatenate([value, value], axis=0)

    first_own = weights.at[pl.ds(LEAD, own)]

    @pl.when(linked)
    def _():
        wait_bytes(first_own, gather_recv.at[LINK - 1])
        for target in range(subs):
            remote(
                weights.at[pl.ds(LEAD, TILE)], follow,
                edge_send.at[target], edge_recv, row - 1, target,
            ).start()

    @pl.loop(0, slots)
    def _(s):
        pltpu.make_async_copy(blocks_ref.at[s], held.at[s], load_sem.at[s]).wait()
        turned[s] = held[s].T

    for offset in range(1, subs):
        theirs = weights.at[pl.ds(pl.multiple_of(LEAD + ring(subs - offset) * own, TILE), own)]
        if offset == LINK:

            @pl.when(jnp.logical_not(linked))
            def _():
                wait_bytes(theirs, gather_recv.at[offset - 1])
        else:
            wait_bytes(theirs, gather_recv.at[offset - 1])

    top = lax.broadcasted_iota(jnp.int32, (TILE, LANES), 0) < PIECES
    inner = weights[LEAD : LEAD + group, :]
    alive = inner > 0.0
    totals = []
    lane = lax.broadcasted_iota(jnp.int32, (1, LANES), 1)
    kept = jnp.sum(jnp.sum(own_live, axis=0, keepdims=True), axis=1, keepdims=True)

    def blocked(start):
        return jnp.concatenate(
            [weights[pl.ds(LEAD + start + q, PAD, stride=PIECES), :] for q in range(PIECES)], axis=1
        )

    def operand(start):
        value = blocked(start)
        high = value.astype(jnp.bfloat16)
        low = (value - high.astype(jnp.float32)).astype(jnp.bfloat16)
        return jnp.concatenate([high, low], axis=0)

    def wide(mask):
        return jnp.concatenate([mask] * PIECES, axis=1)

    def dot(left, right):
        return lax.dot_general(left, right, (((1,), (0,)), ((), ())), preferred_element_type=jnp.float32)

    edge_rows = pl.ds(group, TILE)
    last_slots = min(LATE, slots - 1)

    for k in range(ITERS):
        final = k == ITERS - 1
        here, lower, upper = operand(0), operand(-PIECES), operand(PIECES)
        first = dot(wide(mask_a[0] + mask_e[...]) * here + wide(mask_c[0]) * lower, held[order[0]])
        total = first * (1.0 - leaving)
        for s in range(1, slots):
            if s == slots - last_slots:
                if k == 0:

                    @pl.when(has_after)
                    def _():
                        wait_bytes(follow, edge_recv)

                    back = jnp.where(top, follow[...], 0.0)
                    back_live = back > 0.0
                else:

                    @pl.when(has_after)
                    def _():
                        wait_bytes(after.at[k - 1], after_recv.at[k - 1])

                    @pl.when(has_before)
                    def _():
                        wait_bytes(before.at[k - 1], before_recv.at[k - 1])

                    back = jnp.where(back_live, 1.0 / (back_sums + jnp.sum(after[k - 1], axis=0)), 0.0)
                    front = front_sums + jnp.where(top, jnp.sum(before[k - 1], axis=0), 0.0)
                    front = jnp.where(alive[:TILE], 1.0 / front, 0.0)
                    inner = jnp.concatenate([front, inner[TILE:]], axis=0)
                    weights[LEAD : LEAD + TILE, :] = front
                weights[LEAD + group : LEAD + span, :] = back
                whole = jnp.concatenate([inner, back], axis=0)
                here, lower, upper = operand(0), operand(-PIECES), operand(PIECES)
            on = wide(mask_a[s]) * here
            total += dot(on + wide(mask_c[s]) * lower, held[order[s]])
            total += dot(on + wide(mask_r[s]) * upper, turned[order[s]])
            if s == 1:
                out = (first[PAD - 1 : PAD] + first[2 * PAD - 1 : 2 * PAD]) * leaving
                for q in range(PIECES):
                    part[k, group + q : group + q + 1, :] = out[:, q * LANES : (q + 1) * LANES]

                if k == 0:

                    @pl.when(has_after)
                    def _():
                        pl.semaphore_wait(ready, 1)

                    if stages:
                        tell(0)

                if not final:
                    for offset in others:
                        remote(
                            part.at[k, edge_rows], peers.at[k, offset - 1, edge_rows],
                            peer_send.at[k], peer_recv.at[k], row, ring(offset),
                        ).start()

                @pl.when(has_after)
                def _():
                    if final:
                        remote(
                            part.at[k, edge_rows], last_before.at[sub], before_send.at[k], before_recv.at[k], row + 1, 0
                        ).start()
                    else:
                        for offset in range(subs):
                            remote(
                                part.at[k, edge_rows], before.at[k, offset], before_send.at[k], before_recv.at[k],
                                row + 1, ring(offset),
                            ).start()

        total += dot(wide(mask_a[0]) * here + wide(mask_r[0]) * upper, turned[order[0]])
        total = total[:PAD] + total[PAD:]

        def keep():
            for q in range(PIECES):
                part[k, pl.ds(q, PAD, stride=PIECES), :] = total[:, q * LANES : (q + 1) * LANES]

        if not final:
            keep()
            for offset in others:
                remote(
                    part.at[k, pl.ds(0, group)], peers.at[k, offset - 1, pl.ds(0, group)],
                    peer_send.at[k], peer_recv.at[k], row, ring(offset),
                ).start()

            @pl.when(has_before)
            def _():
                for offset in range(subs):
                    remote(
                        part.at[k, pl.ds(0, TILE)], after.at[k, offset], after_send.at[k], after_recv.at[k],
                        row - 1, ring(offset),
                    ).start()

            if k < stages:
                hear(k)
            if k + 1 < stages:
                tell(k + 1)
            product = whole * part[k, 0:span, :]
            totals.append(jnp.sum(jnp.sum(product, axis=0, keepdims=True), axis=1, keepdims=True))
            if k == 0:
                for offset in range(1, subs):
                    wait_bytes(weights.at[mine], gather_send.at[offset - 1])

                @pl.when(linked)
                def _():
                    for target in range(subs):
                        wait_bytes(weights.at[pl.ds(LEAD, TILE)], edge_send.at[target])

            wait_bytes(peers.at[k], peer_recv.at[k])
            sums = part[k, 0:span, :]
            for offset in range(1, subs):
                sums += peers[k, offset - 1]
            front_sums, back_sums = sums[:TILE], sums[group:]
            inner = jnp.where(alive, 1.0 / sums[:group], 0.0)
            weights[LEAD : LEAD + group, :] = inner
        else:
            scalars = jnp.zeros((1, LANES), jnp.float32)
            for i, value in enumerate(totals + [kept]):
                scalars = jnp.where(lane == i, value, scalars)
            sums_out[1:2, :] = scalars
            for j in range(k, stages):
                hear(j)
                if j + 1 < stages:
                    tell(j + 1)
            product = back * part[k, group:span, :]
            blocked_product = blocked(0) * total
            for q in range(PIECES):
                product += blocked_product[:, q * LANES : (q + 1) * LANES]
            sums_out[0:1, :] = jnp.sum(product, axis=0, keepdims=True)

            keep()
            for offset in others:
                theirs = pl.ds(pl.multiple_of(ring(offset) * own, TILE), own)
                remote(
                    part.at[k, theirs], last_peers.at[offset - 1], peer_send.at[k], peer_recv.at[k], row, ring(offset)
                ).start()

            @pl.loop(0, rows)
            def _(target_row):
                for offset in others:
                    remote(
                        sums_out, sums_in.at[row * subs + offset], sums_send, sums_recv, target_row, ring(offset)
                    ).start()

                @pl.when(target_row != row)
                def _():
                    remote(sums_out, sums_in.at[row * subs], sums_send, sums_recv, target_row, sub).start()

            wait_bytes(last_peers, peer_recv.at[k])

            @pl.when(jnp.logical_and(has_before, sub == 0))
            def _():
                wait_bytes(last_before, before_recv.at[k])

            sums = part[k, pl.ds(pl.multiple_of(sub * own, TILE), own), :] + jnp.sum(last_peers[...], axis=0)
            front = jnp.where(top, jnp.sum(last_before[...], axis=0), 0.0)
            if own > TILE:
                front = jnp.concatenate([front, jnp.zeros((own - TILE, LANES), jnp.float32)], axis=0)
            sums = sums + front
            now = weights[mine, :]
            inverse = jnp.where(own_live > 0.0, 1.0 / sums, 0.0)
            scaled = now * sums
            everyone = sums_in.at[pl.ds(0, devices - 1)]
            sums_in[row * subs] = sums_out[...]
            wait_bytes(everyone, sums_recv)
            grand = [sums_in[i] for i in range(4)]
            for i in range(4, devices):
                grand[i % 4] = grand[i % 4] + sums_in[i]
            grand = (grand[0] + grand[1]) + (grand[2] + grand[3])
            bins = grand[1:2, ITERS - 1 : ITERS]
            all_scaled = jnp.sum(grand[0:1], axis=1, keepdims=True)
            scale = all_scaled / bins
            for i in range(ITERS - 1):
                scale = scale * (grand[1:2, i : i + 1] / bins)
            both_ref[1] = scaled * (bins / all_scaled)
            both_ref[0] = scale * inverse

    for k in range(ITERS):
        final = k == ITERS - 1
        wait_bytes(last_peers if final else peers.at[k], peer_send.at[k])

        @pl.when(has_after)
        def _():
            wait_bytes(last_before.at[0] if final else before.at[k], before_send.at[k])

        if not final:

            @pl.when(has_before)
            def _():
                wait_bytes(after.at[k], after_send.at[k])

    wait_bytes(sums_in.at[pl.ds(0, devices - 1)], sums_send)


def shards(blocks, blk_row, blk_col, counts, bias, mask):
    rows, subs = lax.axis_size("row"), lax.axis_size("sub")
    slots = blocks.shape[0]
    own = bias.shape[0] // LANES
    group = own * subs
    span = group + TILE
    mid = ITERS - 1
    f32, bf16 = jnp.float32, jnp.bfloat16
    dma = pltpu.SemaphoreType.DMA
    vmem = pl.BlockSpec(memory_space=pltpu.VMEM)
    def pin(x):
        return pltpu.with_memory_space_constraint(x, pltpu.HBM)

    both = pl.pallas_call(
        kernel,
        out_shape=pltpu.VMEM((2, own, LANES), f32),
        in_specs=[pl.BlockSpec(memory_space=pltpu.HBM)] * 6,
        out_specs=vmem,
        scratch_shapes=[
            pltpu.SMEM((slots,), jnp.int32),
            pltpu.SMEM((slots,), jnp.int32),
            pltpu.SMEM((1,), jnp.int32),
            pltpu.VMEM((own, LANES), f32),
            pltpu.VMEM((own, LANES), jnp.int32),
            pltpu.VMEM(blocks.shape, bf16),
            pltpu.VMEM(blocks.shape, bf16),
            pltpu.VMEM((LEAD + PAD * PIECES + TILE, LANES), f32),
            pltpu.VMEM((TILE, LANES), f32),
            pltpu.VMEM((ITERS, span, LANES), f32),
            pltpu.VMEM((mid, subs - 1, span, LANES), f32),
            pltpu.VMEM((mid, subs, TILE, LANES), f32),
            pltpu.VMEM((mid, subs, TILE, LANES), f32),
            pltpu.VMEM((subs - 1, own, LANES), f32),
            pltpu.VMEM((subs, TILE, LANES), f32),
            pltpu.VMEM((2, LANES), f32),
            pltpu.VMEM((rows * subs, 2, LANES), f32),
            pltpu.VMEM((slots, 2 * PAD, LANES), bf16),
            pltpu.VMEM((slots, 2 * PAD, LANES), bf16),
            pltpu.VMEM((slots, 2 * PAD, LANES), bf16),
            pltpu.VMEM((2 * PAD, LANES), bf16),
            dma((5,)),
            dma((slots,)),
            dma((subs - 1,)),
            dma((subs - 1,)),
            dma((subs,)),
            dma,
            dma((ITERS,)),
            dma((ITERS,)),
            dma((ITERS,)),
            dma((ITERS,)),
            dma((mid,)),
            dma((mid,)),
            dma,
            dma,
            pltpu.SemaphoreType.REGULAR((max((rows - 1).bit_length(), 1),)),
            pltpu.SemaphoreType.REGULAR,
        ],
        compiler_params=pltpu.CompilerParams(
            collective_id=0, has_side_effects=True, vmem_limit_bytes=40 * 1024 * 1024
        ),
    )(pin(blk_row), pin(blk_col), counts, pin(bias.reshape(own, LANES)), pin(mask.reshape(own, LANES)), pin(blocks))
    balanced, coverage = both[0], both[1]
    return balanced.reshape(-1), coverage.reshape(-1)


def solution(mesh):
    everywhere = P(("row", "sub"))
    return jax.shard_map(
        shards,
        mesh=mesh,
        in_specs=(P(("row", "sub"), None, None),) + (everywhere,) * 5,
        out_specs=(everywhere, everywhere),
        check_vma=False,
    )
```
